256 devices in a mesh: dp: 16 (over x_hi, z), tm: 16 (over x_lo, y, core).
Axes of the slice: x: 4 (x_hi: 2, x_lo: 2; x = x_hi * 2 + x_lo), y: 4, z: 8, core: 2. Of those that a mesh axis runs over, the one named last changes fastest.
Arguments:
- tokens: bfloat16 [16, 256, 48, 1152], P('dp', 'tm'), may hold values from -6 to 6
- mod_scale: float32 [16, 1152], P('dp'), may hold values from -0.5 to 0.5
- mod_gate: float32 [16, 1152], P('dp'), may hold values from 0.3 to 3
- w_qkv: bfloat16 [1152, 1728], P('tm'), may hold values from -3 to 3
- w_out: bfloat16 [1152, 576], P('tm'), may hold values from -0.25 to 0.25
- d_out: bfloat16 [16, 256, 48, 1152], P('dp', 'tm'), may hold values from -6 to 6
Outputs:
- d_tokens: bfloat16 [16, 256, 48, 1152], P('dp', 'tm')
- d_w_qkv: float32 [1152, 1728], P('tm', 'dp')
- d_w_out: float32 [1152, 576], P('tm', 'dp')
The draws below stay inside these ranges and needn't reach their ends.
All inputs are finite; a program needn't handle non-finite values.
Results may differ from the reference program's by a relative error of at most 0.011.
Values may be sent and summed in bfloat16 or wider, within the bound.
A program may use at most 128 MiB of HBM per device.

```python
import math
import jax
import jax.numpy as jnp
from jax import lax

D = 1152
HEADS = 8
HD = 576
FRAMES = 256
PATCH = 48
CLIPS = 16
N_DP = 16


def draw_w_qkv(key, part):
    key = jax.random.fold_in(key, 7)
    first_key = jax.random.fold_in(key, 0)
    normal_part = jax.random.normal(first_key, (D, 3 * HD), jnp.float32) * D ** (-0.5)
    return jnp.clip(normal_part, -3.0, 3.0).astype(jnp.bfloat16)


def shard_levels(stream_key, dims, shards, low, top_value):
    loudness = 1.0
    for position, parts in shards:
        draws = jax.random.uniform(jax.random.fold_in(jax.random.fold_in(stream_key, 6), position), (parts,), jnp.float32, low / len(shards), top_value / len(shards))
        loudness = loudness * jnp.repeat(jnp.exp(draws), dims[position] // parts).reshape((-1,) + (1,) * (len(dims) - 1 - position))
    return loudness


def centred(stream_key, dims, spread, reach, shards=(), dtype=jnp.bfloat16):
    gain = shard_levels(stream_key, dims, shards, -0.22, 0.18) if shards else 1.0
    entries = jax.random.normal(stream_key, dims, jnp.float32) * spread * gain
    return jnp.minimum(jnp.maximum(entries, -reach), reach).astype(dtype)


def setup_inputs(seed: int = 0) -> dict:
    splits = jax.random.split(jax.random.key(seed), 7)
    tokens = centred(splits[0], (CLIPS, FRAMES, PATCH, D), 1.0, 6.0, ((0, 16), (1, 16)))
    mod_scale = jnp.clip(jax.random.uniform(splits[1], (CLIPS, D), jnp.float32, -0.5, 0.5) * shard_levels(splits[1], (CLIPS, D), ((0, 16),), -0.4, 0.0), -0.5, 0.5)
    mod_gate = jnp.clip(jnp.exp(math.log(3.0) - 2.3025851 * jax.random.uniform(splits[2], (CLIPS, D), jnp.float32) ** shard_levels(splits[2], (CLIPS, D), ((0, 16),), -0.2, 0.2)), 0.3, 3.0)
    w_qkv = draw_w_qkv(jax.random.fold_in(splits[6], 71), 0)
    w_out = centred(splits[4], (D, HD), HD ** -0.5, 0.25, ((0, 16),))
    d_out = centred(splits[5], (CLIPS, FRAMES, PATCH, D), 1.0, 6.0, ((0, 16), (1, 16)))
    return dict(tokens=tokens, mod_scale=mod_scale, mod_gate=mod_gate, w_qkv=w_qkv, w_out=w_out, d_out=d_out)


EPS = 1e-06

def mixing(form, left, right):
    return jnp.einsum(form, left.astype(jnp.float32), right.astype(jnp.float32))

def normalize_rows(rows, scale_vec):
    values = rows.astype(jnp.float32)
    centered = values - lax.optimization_barrier(jnp.mean(values, axis=-1, keepdims=True))
    inverse_std = lax.rsqrt(lax.optimization_barrier(jnp.mean(centered * centered, axis=-1, keepdims=True)) + EPS)
    unit_rows = centered * inverse_std
    modulated = (unit_rows * (1.0 + scale_vec)).astype(jnp.bfloat16)
    return (modulated, unit_rows, inverse_std)

def attention_grads(projected, attn_grad, head_count):
    frames, patches, width = projected.shape
    head_dim = width // (3 * head_count)
    split_view = projected.reshape(frames, patches, 3, head_count, head_dim)
    queries = split_view[:, :, 0]
    keys_all = split_view[:, :, 1]
    values_all = split_view[:, :, 2]
    factor = 1.0 / math.sqrt(head_dim)
    grad_view = attn_grad.reshape(frames, patches, head_count, head_dim)
    scores = mixing('fphd,gphd->phfg', queries, keys_all) * factor
    highest = lax.optimization_barrier(jnp.max(scores, axis=-1, keepdims=True))
    expo = jnp.exp(scores - highest)
    probs = expo / lax.optimization_barrier(jnp.sum(expo, axis=-1, keepdims=True))
    probs_low = probs.astype(jnp.bfloat16)
    attended = mixing('phfg,gphd->fphd', probs_low, values_all).astype(jnp.bfloat16)
    prob_grad = mixing('fphd,gphd->phfg', grad_view, values_all)
    value_grad = mixing('phfg,fphd->gphd', probs_low, grad_view).astype(jnp.bfloat16)
    score_grad = (probs * (prob_grad - lax.optimization_barrier(jnp.sum(probs * prob_grad, axis=-1, keepdims=True)))).astype(jnp.bfloat16)
    query_grad = (mixing('phfg,gphd->fphd', score_grad, keys_all) * factor).astype(jnp.bfloat16)
    key_grad = (mixing('phfg,fphd->gphd', score_grad, queries) * factor).astype(jnp.bfloat16)
    stacked = jnp.stack([query_grad, key_grad, value_grad], axis=2).reshape(frames, patches, width)
    return (attended.reshape(frames, patches, head_count * head_dim), stacked)

def clip_grads(rows, scale_vec, gate_vec, w_qkv, w_out, d_rows):
    modulated, unit_rows, inverse_std = normalize_rows(rows, scale_vec)
    projected = mixing('fpd,dc->fpc', modulated, w_qkv).astype(jnp.bfloat16)
    branch_grad = (d_rows.astype(jnp.float32) * gate_vec).astype(jnp.bfloat16)
    attn_grad = mixing('fpd,dc->fpc', branch_grad, w_out).astype(jnp.bfloat16)
    attended, proj_grad = attention_grads(projected, attn_grad, HEADS)
    mod_grad = mixing('fpc,dc->fpd', proj_grad, w_qkv)
    unit_grad = mod_grad * (1.0 + scale_vec)
    branch = inverse_std * (unit_grad - lax.optimization_barrier(jnp.mean(unit_grad, axis=-1, keepdims=True)) - unit_rows * lax.optimization_barrier(jnp.mean(unit_grad * unit_rows, axis=-1, keepdims=True)))
    d_rows_out = (d_rows.astype(jnp.float32) + branch).astype(jnp.bfloat16)
    grad_qkv = mixing('fpd,fpc->dc', modulated, proj_grad)
    grad_out = mixing('fpd,fpc->dc', branch_grad, attended)
    return (d_rows_out, grad_qkv, grad_out)

def reference(tokens, mod_scale, mod_gate, w_qkv, w_out, d_out):

    def visit(running, clip_data):
        rows, scale_vec, gate_vec, d_rows = clip_data
        d_rows_out, grad_qkv, grad_out = clip_grads(rows, scale_vec, gate_vec, w_qkv, w_out, d_rows)
        return ((running[0] + grad_qkv, running[1] + grad_out), d_rows_out)
    start = (jnp.zeros((D, 3 * HD), jnp.float32), jnp.zeros((D, HD), jnp.float32))
    totals, d_tokens = lax.scan(visit, start, (tokens, mod_scale, mod_gate, d_out))
    grad_scale = 1.0 / math.sqrt(N_DP * FRAMES * PATCH)
    return (d_tokens, totals[0] * grad_scale, totals[1] * grad_scale)
```

```python
import math

import jax
import jax.numpy as jnp
from jax import lax
from jax.experimental import pallas as pl
from jax.experimental.pallas import tpu as pltpu
from jax.sharding import PartitionSpec as P

F32, BF16 = jnp.float32, jnp.bfloat16
MESH = pl.DeviceIdType.MESH
HEADS, HEAD, PADDED = 8, 72, 80
EPS = 1e-6
D, FR, PATCH, LOCAL = 1152, 256, 48, 16
FACTOR = 1.0 / math.sqrt(HEAD)
EXP2 = FACTOR * math.log2(math.e)
OR = HEADS * PADDED
QR = 3 * OR
ROWS = 768
GRAD_SCALE = 1.0 / math.sqrt(16 * 256 * 48)
TILES = 18


def nn(a, b):
    return lax.dot_general(a, b, (((1,), (0,)), ((), ())), preferred_element_type=F32)


def nt(a, b):
    return lax.dot_general(a, b, (((1,), (1,)), ((), ())), preferred_element_type=F32)


def tn(a, b):
    return lax.dot_general(a, b, (((0,), (0,)), ((), ())), preferred_element_type=F32)


def grid2(shape):
    return lax.broadcasted_iota(jnp.int32, shape, 0), lax.broadcasted_iota(jnp.int32, shape, 1)


def padded(r):
    return lax.div(r, HEAD) * PADDED + lax.rem(r, HEAD)


def onehot(cond):
    return jnp.where(cond, 1.0, 0.0).astype(BF16)


def swap_matrix():
    r, c = grid2((256, 256))
    return onehot(c == lax.rem(r, 16) * 16 + lax.div(r, 16))


def prep_weights(wbuf, wc, wt):
    r, c = grid2((144, 160))
    sel = onehot(c == padded(r))
    for u in range(8):
        for i in range(TILES // 2):
            block = jnp.concatenate(
                [jnp.concatenate([wbuf[2 * i + k, core, u] for k in range(2)], axis=1) for core in range(2)], axis=0
            )
            wc[144 * u : 144 * u + 144, 256 * i : 256 * i + 256] = nn(sel, block).astype(BF16)
    r, c = grid2((160, 256))
    d = lax.rem(r, PADDED)
    target = lax.div(r, PADDED) * HEAD + d
    for j in range(16):
        lo = 128 * ((144 * j) // 128)
        e = onehot((d < HEAD) & (c == target + (144 * j - lo)))
        wt[160 * j : 160 * j + 160, :] = nt(e, wc[:, lo : lo + 256]).astype(BF16)


def head_step(h, p, pt, ot, dp, at):
    def rows(base):
        return pl.ds(pl.multiple_of(base + PADDED * h, 16), PADDED)

    cols = pl.ds(pl.multiple_of(p * FR, FR), FR)
    q, k, v, o = pt[rows(0), :], pt[rows(OR), :], pt[rows(2 * OR), :], ot[rows(0), :]
    s = tn(k, q)
    top = jnp.max(s, axis=0, keepdims=True)
    e = jnp.exp2((s - top) * EXP2)
    probs = e * (1.0 / jnp.sum(e, axis=0, keepdims=True))
    low = probs.astype(BF16)
    pg = tn(v, o)
    ds = (probs * (pg - jnp.sum(probs * pg, axis=0, keepdims=True))).astype(BF16)
    at[rows(0), cols] = nn(v, low).astype(BF16)
    dp[rows(0), cols] = (nn(k, ds) * FACTOR).astype(BF16)
    dp[rows(OR), cols] = (nt(q, ds) * FACTOR).astype(BF16)
    dp[rows(2 * OR), cols] = nt(o, low).astype(BF16)


def patch_step(p, x, g, scale, gate, wt, mod_ref, bg_ref, pt, ot, dp, at, unit_ref, out):
    rows = pl.ds(pl.multiple_of(p * FR, FR), FR)
    values = x[p].astype(F32)
    cen = values - jnp.mean(values, axis=-1, keepdims=True)
    inv = lax.rsqrt(jnp.mean(cen * cen, axis=-1, keepdims=True) + EPS)
    unit = cen * inv
    unit_ref[...] = unit
    mod = (unit * (1.0 + scale)).astype(BF16)
    mod_ref[rows, :] = mod
    pt[...] = nt(wt[0:QR, :], mod).astype(BF16)
    bg = (g[p].astype(F32) * gate).astype(BF16)
    bg_ref[rows, :] = bg
    ot[...] = nt(wt[QR : QR + OR, :], bg).astype(BF16)

    def body(h, carry):
        head_step(h, p, pt, ot, dp, at)
        return carry

    lax.fori_loop(0, HEADS, body, 0, unroll=True)
    ug = tn(dp[:, rows], wt[0:QR, :]) * (1.0 + scale)
    unit = unit_ref[...]
    branch = inv * (
        ug - jnp.mean(ug, axis=-1, keepdims=True) - unit * jnp.mean(ug * unit, axis=-1, keepdims=True)
    )
    out[p] = (g[p].astype(F32) + branch).astype(BF16)


def weight_grads(par, group, mod_ref, bg_ref, dp, at, l1, l2, dw):
    r, c = grid2((112, 160))
    sel1 = onehot((r < 108) & (c == padded(r + 36 * par)))
    r, c = grid2((48, 80))
    sel2 = onehot((r >= 12) & (c == r - 12 + 36 * par))
    for i in range(4):
        half = 4 * (i % 2) + 2 * group + i // 2
        lo = pl.multiple_of(240 * half + 80 * par, 16)
        l1[112 * i : 112 * i + 112, :] = nn(sel1, dp[pl.ds(lo, 160), :]).astype(BF16)
        l2[48 * i : 48 * i + 48, :] = nn(sel2, at[PADDED * half : PADDED * half + PADDED, :]).astype(BF16)
    t1 = nn(l1[...], mod_ref[...])
    t2 = nn(l2[...], bg_ref[...])
    for i in range(4):
        a, b = t1[112 * i : 112 * i + 112], t2[48 * i : 48 * i + 48]
        dw[4 * group + i, 0:96, :] = a[0:96].astype(BF16)
        dw[4 * group + i, 96:112, :] = (a[96:112] + b[0:16]).astype(BF16)
        dw[4 * group + i, 112:144, :] = b[16:48].astype(BF16)


def add(a, b):
    return (a.astype(F32) + b.astype(F32)).astype(BF16)


def wait_bytes(ref, sem):
    pltpu.make_async_copy(ref, ref, sem).wait()


def main_kernel(
    tok, dout, wsrc, scale_ref, gate_ref,
    back, dwq, dwo,
    tok_in, dout_in, tok_tx, dout_tx, x, g, wbuf, wc, wt, mod_ref, bg_ref, pt, ot, dp, at, unit_ref, l1, l2, dtok,
    dw_tx, dw_own, core_rx, up_rx, dn_rx, xh_rx, tm_tx, tm_rx,
    in_sem, w_send, w1_sem, up_sem, dn_sem, wcore_sem, a_send, x_sem, g_sem, back_send, back_sem,
    core_send, core_sem, up_send, dn_send, up_recv, dn_recv, xh_send, xh_sem, tm_send, tm_sem,
):
    tm, dpi = lax.axis_index("tm"), lax.axis_index("dp")
    xl, y, c = lax.div(tm, 8), lax.rem(lax.div(tm, 2), 4), lax.rem(tm, 2)
    xh, z = lax.div(dpi, 8), lax.rem(dpi, 8)
    mine8 = xl * 4 + y

    def peer(a, b, cc):
        return {"tm": lax.rem(xl + a, 2) * 8 + lax.rem(y + b, 4) * 2 + lax.rem(c + cc, 2), "dp": dpi}

    def ring(step):
        return {"tm": tm, "dp": xh * 8 + lax.rem(z + step + 8, 8)}

    partner = peer(0, 0, 1)
    across = {"tm": tm, "dp": lax.rem(dpi + 8, 16)}
    peers = [(a, b, cc) for a in range(2) for b in range(4) for cc in range(2) if (a, b, cc) != (0, 0, 0)]

    def send(src, dst, ssem, rsem, target):
        copy = pltpu.make_async_remote_copy(
            src_ref=src, dst_ref=dst, send_sem=ssem, recv_sem=rsem, device_id=target, device_id_type=MESH
        )
        copy.start()

    in0 = pltpu.make_async_copy(tok, tok_in, in_sem.at[0])
    in1 = pltpu.make_async_copy(dout, dout_in, in_sem.at[1])
    in0.start()
    in1.start()

    barrier = pltpu.get_barrier_semaphore()
    for target in [peer(*o) for o in peers] + [ring(1), ring(-1), across]:
        pl.semaphore_signal(barrier, inc=1, device_id=target, device_id_type=MESH)
    pl.semaphore_wait(barrier, 18)

    first, extra = pl.ds(2 * z, 2), 16 + z
    pltpu.make_async_copy(wsrc.at[first], wbuf.at[first, c, mine8], w1_sem.at[0]).start()
    for a in range(2):
        for b in range(4):
            if (a, b) != (0, 0):
                send(wsrc.at[first], wbuf.at[first, c, mine8], w_send.at[0], w1_sem.at[0], peer(a, b, 0))

    @pl.when(z < 2)
    def _():
        pltpu.make_async_copy(wsrc.at[extra], wbuf.at[extra, c, mine8], w1_sem.at[1]).start()
        for a in range(2):
            for b in range(4):
                if (a, b) != (0, 0):
                    send(wsrc.at[extra], wbuf.at[extra, c, mine8], w_send.at[1], w1_sem.at[1], peer(a, b, 0))

    swap = swap_matrix()
    for n, (src, tx) in enumerate(((tok_in, tok_tx), (dout_in, dout_tx))):
        (in0, in1)[n].wait()
        for b in range(3):
            block = src[:, 16 * b : 16 * b + 16, :].reshape(256, D)
            tx[16 * b : 16 * b + 16] = nn(swap, block).astype(BF16).reshape(16, 16, D)
    mine16 = pl.ds(pl.multiple_of(LOCAL * tm, LOCAL), LOCAL)
    for p in range(3):
        for tx, rx, sem in ((tok_tx, x, x_sem), (dout_tx, g, g_sem)):
            pltpu.make_async_copy(tx.at[3 * tm + p], rx.at[p, mine16], sem.at[p]).start()
            for o in peers:
                target = peer(*o)
                send(tx.at[3 * target["tm"] + p], rx.at[p, mine16], a_send.at[0], sem.at[p], target)

    def pmain(q):
        return wbuf.at[pl.ds(2 * q, 2), c]

    def ptile(q, k):
        return wbuf.at[2 * q + k, c]

    def pextra(q):
        return wbuf.at[16 + q, c]

    wait_bytes(pmain(z), w1_sem.at[0])
    send(pmain(z), pmain(z), w_send.at[2], up_sem.at[0, 0], ring(1))
    send(pmain(z), pmain(z), w_send.at[3], dn_sem.at[0, 0], ring(-1))
    send(pmain(z), pmain(z), w_send.at[4], wcore_sem.at[0], partner)

    @pl.when(z < 2)
    def _():
        wait_bytes(pextra(z), w1_sem.at[1])
        send(pextra(z), pextra(z), w_send.at[5], up_sem.at[0, 1], ring(1))
        send(pextra(z), pextra(z), w_send.at[6], dn_sem.at[0, 1], ring(-1))
        send(pextra(z), pextra(z), w_send.at[7], wcore_sem.at[1], partner)

    for k in range(1, 5):
        for sem, way in ((up_sem, 1), (dn_sem, -1)):
            q = lax.rem(z - way * k + 8, 8)
            if k < 4:
                wait_bytes(pmain(q), sem.at[k - 1, 0])
                if k < 3:
                    send(pmain(q), pmain(q), w_send.at[2 + (way < 0)], sem.at[k, 0], ring(way))
                else:
                    half = ptile(q, int(way < 0))
                    send(half, half, w_send.at[8 + (way < 0)], sem.at[k, 0], ring(way))
                send(pmain(q), pmain(q), w_send.at[4], wcore_sem.at[0], partner)

                @pl.when(q < 2)
                def _():
                    wait_bytes(pextra(q), sem.at[k - 1, 1])
                    if k < 3 or way > 0:
                        send(pextra(q), pextra(q), w_send.at[5 + (way < 0)], sem.at[k, 1], ring(way))
                    send(pextra(q), pextra(q), w_send.at[7], wcore_sem.at[1], partner)
            else:
                half = ptile(q, int(way < 0))
                wait_bytes(half, sem.at[3, 0])
                send(half, half, w_send.at[4], wcore_sem.at[0], partner)
                if way > 0:

                    @pl.when(q < 2)
                    def _():
                        wait_bytes(pextra(q), sem.at[3, 1])
                        send(pextra(q), pextra(q), w_send.at[7], wcore_sem.at[1], partner)

    wait_bytes(wbuf.at[pl.ds(0, 16), 1 - c], wcore_sem.at[0])
    wait_bytes(wbuf.at[pl.ds(16, 2), 1 - c], wcore_sem.at[1])
    prep_weights(wbuf, wc, wt)

    scale, gate = scale_ref[...], gate_ref[...]
    for p in range(3):
        wait_bytes(x.at[p], x_sem.at[p])
        wait_bytes(g.at[p], g_sem.at[p])
        patch_step(p, x, g, scale, gate, wt, mod_ref, bg_ref, pt, ot, dp, at, unit_ref, dtok)
        pltpu.make_async_copy(dtok.at[p, mine16], back.at[3 * tm + p], back_sem.at[0]).start()
        for o in peers:
            target = peer(*o)
            theirs = pl.ds(pl.multiple_of(LOCAL * target["tm"], LOCAL), LOCAL)
            send(dtok.at[p, theirs], back.at[3 * tm + p], back_send.at[0], back_sem.at[0], target)

    for group in range(2):
        weight_grads(1 - c, group, mod_ref, bg_ref, dp, at, l1, l2, dw_tx)
        part = pl.ds(4 * group, 4)
        send(dw_tx.at[part], core_rx.at[part], core_send.at[group], core_sem.at[group], partner)
    for group in range(2):
        weight_grads(c, group, mod_ref, bg_ref, dp, at, l1, l2, dw_own)
    for group in range(2):
        part = pl.ds(4 * group, 4)
        wait_bytes(core_rx.at[part], core_sem.at[group])
        for i in range(4 * group, 4 * group + 4):
            dw_own[i] = add(dw_own[i], core_rx[i])

    even = lax.rem(z + c, 2) == 0

    def unit(step):
        return lax.div(lax.rem(z + step + 8, 8), 2) * 2

    ways = ((1, up_rx, up_send, up_recv), (-1, dn_rx, dn_send, dn_recv))

    @pl.when(even)
    def _():
        for way, rx, ssem, rsem in ways:
            own = unit(4) + int(way < 0)
            send(dw_own.at[own], rx.at[0, int(way < 0)], ssem.at[0], rsem.at[0, int(way < 0)], ring(way))
        for i in range(2):
            for way, rx, ssem, rsem in ways:
                own = unit(2 * way) + i
                wait_bytes(rx.at[0, i], rsem.at[0, i])
                dw_own[own] = add(dw_own[own], rx[0, i])
                send(dw_own.at[own], rx.at[1, i], ssem.at[1 + i], rsem.at[1, i], ring(way))
        for i in range(2):
            own = unit(0) + i
            wait_bytes(up_rx.at[1, i], up_recv.at[1, i])
            wait_bytes(dn_rx.at[1, i], dn_recv.at[1, i])
            dw_own[own] = (
                dw_own[own].astype(F32) + up_rx[1, i].astype(F32) + dn_rx[1, i].astype(F32)
            ).astype(BF16)
        send(dw_own.at[unit(0) + 1 - xh], xh_rx, xh_send.at[0], xh_sem.at[0], across)
        wait_bytes(xh_rx, xh_sem.at[0])
        total = add(dw_own[unit(0) + xh], xh_rx[...])
        dw_own[unit(0) + xh] = total
        r, cl = grid2((80, 256))
        for t in range(16):
            lo = min(128 * ((72 * t) // 128), 896)
            sel = onehot((r < HEAD) & (cl == r + (72 * t - lo)))
            tm_tx[t, :, 0:144] = nt(sel, dw_own[unit(0) + xh, :, lo : lo + 256]).astype(BF16)
        pltpu.make_async_copy(tm_tx.at[tm], tm_rx.at[mine8], tm_sem.at[0]).start()
        for o in peers:
            target = peer(*o)
            send(tm_tx.at[target["tm"]], tm_rx.at[mine8], tm_send.at[0], tm_sem.at[0], target)
        for way, rx, ssem, rsem in ways:
            for n in range(3):
                wait_bytes(dw_own.at[0], ssem.at[n])
        wait_bytes(xh_rx, xh_send.at[0])
        wait_bytes(tm_tx.at[pl.ds(0, 15)], tm_send.at[0])

    @pl.when(jnp.logical_not(even))
    def _():
        for way, rx, ssem, rsem in ways:
            i = int(way < 0)
            own = unit(3 * way) + i
            wait_bytes(rx.at[0, i], rsem.at[0, i])
            dw_own[own] = add(dw_own[own], rx[0, i])
            send(dw_own.at[own], rx.at[0, i], ssem.at[0], rsem.at[0, i], ring(way))
        for way, rx, ssem, rsem in ways:
            i = int(way > 0)
            send(dw_own.at[unit(3 * way) + i], rx.at[0, i], ssem.at[1], rsem.at[0, i], ring(way))
        for i in range(2):
            for way, rx, ssem, rsem in ways:
                own = unit(way) + i
                wait_bytes(rx.at[1, i], rsem.at[1, i])
                dw_own[own] = add(dw_own[own], rx[1, i])
                send(dw_own.at[own], rx.at[1, i], ssem.at[2 + i], rsem.at[1, i], ring(way))
        for way, rx, ssem, rsem in ways:
            for n in range(4):
                wait_bytes(dw_own.at[0], ssem.at[n])

    wait_bytes(tm_rx, tm_sem.at[0])
    total = tm_rx[0].astype(F32)
    for i in range(1, 8):
        total = total + tm_rx[i].astype(F32)
    total = total * GRAD_SCALE
    dwq[...] = total[0:HEAD, 0:108]
    dwo[...] = total[0:HEAD, 108:144]

    wait_bytes(back, back_sem.at[0])
    wait_bytes(tok_tx.at[pl.ds(0, 45)], a_send.at[0])
    wait_bytes(tok_tx.at[pl.ds(0, 45)], a_send.at[0])
    wait_bytes(tok_tx.at[pl.ds(0, 45)], back_send.at[0])
    for group in range(2):
        wait_bytes(core_rx.at[pl.ds(0, 4)], core_send.at[group])
    wait_bytes(wbuf.at[pl.ds(0, 2), 0, pl.ds(0, 7)], w_send.at[0])
    for n in (2, 3):
        wait_bytes(wbuf.at[pl.ds(0, 6), 0], w_send.at[n])
    wait_bytes(wbuf.at[pl.ds(0, 16), 0], w_send.at[4])
    for n in (8, 9):
        wait_bytes(wbuf.at[0, 0], w_send.at[n])

    @pl.when(z < 2)
    def _():
        wait_bytes(wbuf.at[0, 0, pl.ds(0, 7)], w_send.at[1])

    for n, steps in ((5, (0, -1, -2, -3)), (6, (0, 1, 2))):
        for s in steps:
            @pl.when(lax.rem(z + s + 8, 8) < 2)
            def _():
                wait_bytes(wbuf.at[0, 0], w_send.at[n])
    wait_bytes(wbuf.at[pl.ds(0, 2), 0], w_send.at[7])


def main_call(tok, dout, wsrc, scale, gate):
    vmem, anyspace = pl.BlockSpec(memory_space=pltpu.VMEM), pl.BlockSpec(memory_space=pl.ANY)
    dma = pltpu.SemaphoreType.DMA
    rows3 = pltpu.VMEM((3, FR, D), BF16)
    sent = pltpu.VMEM((PATCH, LOCAL, D), BF16)
    chunks = pltpu.VMEM((8, 144, D), BF16)
    passed = pltpu.VMEM((2, 2, 144, D), BF16)
    return pl.pallas_call(
        main_kernel,
        out_shape=(
            jax.ShapeDtypeStruct((PATCH, LOCAL, D), BF16),
            jax.ShapeDtypeStruct((HEAD, 108), F32),
            jax.ShapeDtypeStruct((HEAD, 36), F32),
        ),
        in_specs=[anyspace, anyspace, anyspace, vmem, vmem],
        out_specs=(anyspace, vmem, vmem),
        scratch_shapes=[
            pltpu.VMEM((LOCAL, PATCH, D), BF16), pltpu.VMEM((LOCAL, PATCH, D), BF16), sent, sent, rows3, rows3,
            pltpu.VMEM((TILES, 2, 8, PADDED, 128), BF16), pltpu.VMEM((D, 128 * TILES), BF16),
            pltpu.VMEM((QR + OR, D), BF16), pltpu.VMEM((ROWS, D), BF16), pltpu.VMEM((ROWS, D), BF16),
            pltpu.VMEM((QR, FR), BF16), pltpu.VMEM((OR, FR), BF16),
            pltpu.VMEM((QR, ROWS), BF16), pltpu.VMEM((OR, ROWS), BF16), pltpu.VMEM((FR, D), F32),
            pltpu.VMEM((448, ROWS), BF16), pltpu.VMEM((192, ROWS), BF16), rows3,
            chunks, chunks, chunks, passed, passed, pltpu.VMEM((144, D), BF16),
            pltpu.VMEM((16, 80, 256), BF16), pltpu.VMEM((8, 80, 256), BF16),
            dma((2,)), dma((10,)), dma((2,)), dma((4, 2)), dma((4, 2)), dma((2,)), dma((1,)), dma((3,)), dma((3,)),
            dma((1,)), dma((1,)),
            dma((2,)), dma((2,)), dma((4,)), dma((4,)), dma((2, 2)), dma((2, 2)), dma((1,)), dma((1,)), dma((1,)),
            dma((1,)),
        ],
        compiler_params=pltpu.CompilerParams(
            collective_id=0, has_side_effects=True, vmem_limit_bytes=62 << 20
        ),
        name="main",
    )(tok, dout, wsrc, scale, gate)


def unswap_kernel(src, dst):
    block = src[...].reshape(256, D)
    dst[...] = nn(swap_matrix(), block).astype(BF16).reshape(LOCAL, 16, D)


def unswap(back):
    return pl.pallas_call(
        unswap_kernel,
        grid=(3,),
        out_shape=jax.ShapeDtypeStruct((LOCAL, PATCH, D), BF16),
        in_specs=[pl.BlockSpec((16, LOCAL, D), lambda i: (i, 0, 0))],
        out_specs=pl.BlockSpec((LOCAL, 16, D), lambda i: (0, i, 0)),
        compiler_params=pltpu.CompilerParams(vmem_limit_bytes=16 << 20),
        name="unswap",
    )(back)


def shards(tokens, mod_scale, mod_gate, w_qkv, w_out, d_out):
    w = jnp.concatenate([w_qkv, w_out], axis=1)
    w = jnp.pad(w, ((0, PADDED - HEAD), (0, 0))).reshape(PADDED, TILES, 128).transpose(1, 0, 2)
    back, dwq, dwo = main_call(tokens[0], d_out[0], w, mod_scale, mod_gate)
    return unswap(back)[None], dwq, dwo


def solution(mesh):
    return jax.shard_map(
        shards,
        mesh=mesh,
        in_specs=(
            P("dp", "tm", None, None),
            P("dp", None),
            P("dp", None),
            P("tm", None),
            P("tm", None),
            P("dp", "tm", None, None),
        ),
        out_specs=(P("dp", "tm", None, None), P("tm", "dp"), P("tm", "dp")),
        check_vma=False,
    )
```

```python
import math

import jax
import jax.numpy as jnp
from jax import lax
from jax.experimental import pallas as pl
from jax.experimental.pallas import tpu as pltpu
from jax.sharding import PartitionSpec as P

F32, BF16 = jnp.float32, jnp.bfloat16
MESH = pl.DeviceIdType.MESH
HEADS, HEAD, PADDED = 8, 72, 80
EPS = 1e-6
D, FR, PATCH, LOCAL = 1152, 256, 48, 16
FACTOR = 1.0 / math.sqrt(HEAD)
EXP2 = FACTOR * math.log2(math.e)
OR = HEADS * PADDED
QR = 3 * OR
ROWS = 768
GRAD_SCALE = 1.0 / math.sqrt(16 * 256 * 48)
TILES = 18


def nn(a, b):
    return lax.dot_general(a, b, (((1,), (0,)), ((), ())), preferred_element_type=F32)


def nt(a, b):
    return lax.dot_general(a, b, (((1,), (1,)), ((), ())), preferred_element_type=F32)


def tn(a, b):
    return lax.dot_general(a, b, (((0,), (0,)), ((), ())), preferred_element_type=F32)


def grid2(shape):
    return lax.broadcasted_iota(jnp.int32, shape, 0), lax.broadcasted_iota(jnp.int32, shape, 1)


def padded(r):
    return lax.div(r, HEAD) * PADDED + lax.rem(r, HEAD)


def onehot(cond):
    return jnp.where(cond, 1.0, 0.0).astype(BF16)


def swap_matrix():
    r, c = grid2((256, 256))
    return onehot(c == lax.rem(r, 16) * 16 + lax.div(r, 16))


def combine(raw, own_w):
    r, c = grid2((144, 160))
    sel = onehot(c == padded(r))
    for i in range(TILES // 2):
        block = jnp.concatenate([raw[core, :, 256 * i : 256 * i + 256] for core in range(2)], axis=0)
        out = nn(sel, block).astype(BF16)
        for k in range(2):
            own_w[288 * i + 144 * k : 288 * i + 144 * k + 144, :] = out[:, 128 * k : 128 * k + 128]


def prep_weights(half, wbuf, wt):
    r, c = grid2((160, 256))
    d = lax.rem(r, PADDED)
    target = lax.div(r, PADDED) * HEAD + d
    for j in range(8 * half, 8 * half + 8):
        tile = (144 * j) // 128
        e = onehot((d < HEAD) & (c == target + (144 * j - 128 * tile)))
        block = jnp.concatenate(
            [
                jnp.concatenate([wbuf[u, 144 * t : 144 * t + 144, :] for t in (tile, tile + 1)], axis=1)
                for u in range(8)
            ],
            axis=0,
        )
        wt[160 * j : 160 * j + 160, :] = nt(e, block).astype(BF16)


def head_step(h, p, pt, ot, dp, at):
    def rows(base):
        return pl.ds(pl.multiple_of(base + PADDED * h, 16), PADDED)

    cols = pl.ds(pl.multiple_of(p * FR, FR), FR)
    q, k, v, o = pt[rows(0), :], pt[rows(OR), :], pt[rows(2 * OR), :], ot[rows(0), :]
    s = tn(k, q)
    top = jnp.max(s, axis=0, keepdims=True)
    e = jnp.exp2((s - top) * EXP2)
    probs = e * (1.0 / jnp.sum(e, axis=0, keepdims=True))
    low = probs.astype(BF16)
    pg = tn(v, o)
    ds = (probs * (pg - jnp.sum(probs * pg, axis=0, keepdims=True))).astype(BF16)
    at[rows(0), cols] = nn(v, low).astype(BF16)
    dp[rows(0), cols] = (nn(k, ds) * FACTOR).astype(BF16)
    dp[rows(OR), cols] = (nt(q, ds) * FACTOR).astype(BF16)
    dp[rows(2 * OR), cols] = nt(o, low).astype(BF16)


def flip(dst, src, cols):
    eye = onehot(jnp.equal(*grid2((256, 256))))
    for lo in range(0, D, 256):
        n = min(256, D - lo)
        dst[lo : lo + n, cols] = nt(eye[:n, :n], src[:, lo : lo + n]).astype(BF16)


def patch_front(p, x, g, scale, gate, wt, mod_ref, bg_ref, mod_flip, bg_flip, pt, ot, unit_ref):
    rows = pl.ds(FR * p, FR)
    values = x[p].astype(F32)
    cen = values - jnp.mean(values, axis=-1, keepdims=True)
    inv = lax.rsqrt(jnp.mean(cen * cen, axis=-1, keepdims=True) + EPS)
    unit = cen * inv
    unit_ref[...] = unit
    mod = (unit * (1.0 + scale)).astype(BF16)
    mod_ref[rows, :] = mod
    flip(mod_flip, mod, rows)
    pt[...] = nt(wt[0:QR, :], mod).astype(BF16)
    bg = (g[p].astype(F32) * gate).astype(BF16)
    bg_ref[rows, :] = bg
    flip(bg_flip, bg, rows)
    ot[...] = nt(wt[QR : QR + OR, :], bg).astype(BF16)
    return inv


def patch_end(p, g, scale, wt, dp, unit_ref, inv, out):
    ug = tn(dp[:, pl.ds(FR * p, FR)], wt[0:QR, :]) * (1.0 + scale)
    unit = unit_ref[...]
    branch = inv * (
        ug - jnp.mean(ug, axis=-1, keepdims=True) - unit * jnp.mean(ug * unit, axis=-1, keepdims=True)
    )
    out[p] = (g[p].astype(F32) + branch).astype(BF16)


def pack_by_column(ks, cols, dp, at, l1, l2):
    r, c = grid2((112, 160))
    r2, c2 = grid2((48, 80))
    for i, k in enumerate(ks):
        odd, half = lax.rem(k, 2), lax.div(k, 2)
        sel = onehot((r < 108) & (c == padded(r + 36 * odd)))
        rows = pl.ds(pl.multiple_of(240 * half + 80 * odd, 16), 160)
        l1[112 * i : 112 * i + 112, cols] = nn(sel, dp[rows, :]).astype(BF16)
        sel = onehot((r2 >= 12) & (c2 == r2 - 12 + 36 * odd))
        rows = pl.ds(pl.multiple_of(80 * half, 16), 80)
        l2[48 * i : 48 * i + 48, cols] = nn(sel, at[rows, :]).astype(BF16)


def grads_by_column(group, l1, l2, mods, bgs, dw):
    a_rows, b_rows = pl.ds(448 * group, 448), pl.ds(192 * group, 192)
    t1 = nn(l1[a_rows, 0:ROWS], mods[0][...]) + nn(l1[a_rows, ROWS:], mods[1][...])
    t2 = nn(l2[b_rows, 0:ROWS], bgs[0][...]) + nn(l2[b_rows, ROWS:], bgs[1][...])
    for i in range(4):
        a, b, row = t1[112 * i : 112 * i + 112], t2[48 * i : 48 * i + 48], 144 * (4 * group + i)
        dw[row : row + 96, :] = a[0:96].astype(BF16)
        dw[row + 96 : row + 112, :] = (a[96:112] + b[0:16]).astype(BF16)
        dw[row + 112 : row + 144, :] = b[16:48].astype(BF16)


def pack_columns(first, cols, dp, first_at, at, lb1, lb2):
    r, c = grid2((144, 160))
    sel = onehot(c == padded(r))
    for i in range(6):
        lo = first + 160 * i
        lb1[144 * i : 144 * i + 144, cols] = nn(sel, dp[lo : lo + 160, :]).astype(BF16)
    lb1[864:896, cols] = jnp.zeros((32, ROWS), BF16)
    lb2[0:96, cols] = jnp.zeros((96, ROWS), BF16)
    for i in range(2):
        lo = first_at + 160 * i
        lb2[96 + 144 * i : 240 + 144 * i, cols] = nn(sel, at[lo : lo + 160, :]).astype(BF16)


def grads_by_row(block, lb1, lb2, mods, bgs, dw):
    rows = pl.ds(pl.multiple_of(288 * block, 16), 288)
    a = nt(mods[0][rows, :], lb1[:, 0:ROWS]) + nt(mods[1][rows, :], lb1[:, ROWS:])
    b = nt(bgs[0][rows, :], lb2[:, 0:ROWS]) + nt(bgs[1][rows, :], lb2[:, ROWS:])
    dw[rows, 0:768] = a[:, 0:768].astype(BF16)
    dw[rows, 768:896] = (a[:, 768:896] + b[:, 0:128]).astype(BF16)
    dw[rows, 896:D] = b[:, 128:384].astype(BF16)


def slice_window(t):
    return min(128 * ((72 * t) // 128), 896)


def column_windows(k):
    return 128 * ((108 * k) // 128), min(128 * ((864 + 36 * k) // 128), 896)


def selections(sel_slice, sel_chunk, sel_rest):
    r, c = grid2((80, 256))
    for t in range(16):
        sel_slice[t] = onehot((r < HEAD) & (c == r + (72 * t - slice_window(t))))
    r, c = grid2((256, 128))
    rt, ct = grid2((16, 256))
    for k in range(8):
        lo1, lo2 = column_windows(k)
        sel_chunk[k, 0:256] = onehot((c < 108) & (r + lo1 == 108 * k + c))
        sel_chunk[k, 256:512] = onehot((c >= 108) & (r + lo2 == 756 + 36 * k + c))
        sel_rest[k] = onehot(ct + lo2 == 756 + 36 * k + 128 + rt)


def add(a, b):
    return (a.astype(F32) + b.astype(F32)).astype(BF16)


def wait_bytes(ref, sem):
    pltpu.make_async_copy(ref, ref, sem).wait()


def main_kernel(
    tok, dout, wq, wo, scale_ref, gate_ref,
    out, dwq, dwo,
    staged, tok_tx, dout_tx, x, g, raw, own_w, wbuf, dw, wt, mod_ref, bg_ref, mod_flip, bg_flip, pt, ot, dp, at,
    unit_ref, l1, l2, dtok, back, mod_rx, bg_rx, mod_flip_rx, bg_flip_rx, dp_rx, at_rx,
    rs_rx, sel_slice, sel_chunk, sel_rest, last_tx, last_rx,
    in_sem, raw_send, raw_sem, w_send, w1_sem, up_sem, dn_sem, wcore_sem, a_send, x_sem, g_sem, back_send, back_sem,
    out_sem, core_send, core_sem, rs_send, rs_sem, last_send, last_sem,
):
    tm, dpi = lax.axis_index("tm"), lax.axis_index("dp")
    xl, y, c = lax.div(tm, 8), lax.rem(lax.div(tm, 2), 4), lax.rem(tm, 2)
    xh, z = lax.div(dpi, 8), lax.rem(dpi, 8)
    mine8 = xl * 4 + y

    def peer(a, b, cc):
        return {"tm": lax.rem(xl + a, 2) * 8 + lax.rem(y + b, 4) * 2 + lax.rem(c + cc, 2), "dp": dpi}

    def ring(step):
        return {"tm": tm, "dp": xh * 8 + lax.rem(z + step + 8, 8)}

    partner = peer(0, 0, 1)
    peers = [(a, b, cc) for a in range(2) for b in range(4) for cc in range(2) if (a, b, cc) != (0, 0, 0)]

    def send(src, dst, ssem, rsem, target):
        copy = pltpu.make_async_remote_copy(
            src_ref=src, dst_ref=dst, send_sem=ssem, recv_sem=rsem, device_id=target, device_id_type=MESH
        )
        copy.start()

    def share(h, q):
        return pl.ds(pl.multiple_of(1296 * h + 160 * q, 16), 160)

    def rest(h):
        return pl.ds(1296 * h + 1280, 16)

    first_in = pltpu.make_async_copy(tok, staged, in_sem.at[0])
    first_in.start()

    barrier = pltpu.get_barrier_semaphore()
    other = {"dp": lax.rem(dpi + 8, 16)}
    greeted = [peer(*o) for o in peers] + [peer(0, 0, 0) | other] + [peer(*o) | other for o in peers]
    for step in range(1, 8):
        for cc in range(2):
            here = {"tm": lax.div(tm, 2) * 2 + lax.rem(c + cc, 2)}
            greeted += [here | {"dp": h * 8 + lax.rem(z + step, 8)} for h in range(2)]
    for target in greeted:
        pl.semaphore_signal(barrier, inc=1, device_id=target, device_id_type=MESH)

    swap = swap_matrix()
    raw[c, 0:HEAD, 0:1728] = wq[...]
    raw[c, 0:HEAD, 1728:2304] = wo[...]
    raw[c, HEAD:PADDED, :] = jnp.zeros((PADDED - HEAD, 2304), BF16)
    for n, tx in enumerate((tok_tx, dout_tx)):
        if n:
            second_in = pltpu.make_async_copy(dout, staged, in_sem.at[1])
            second_in.start()
            second_in.wait()
        else:
            first_in.wait()
        for b in range(3):
            block = staged[:, 16 * b : 16 * b + 16, :].reshape(256, D)
            tx[16 * b : 16 * b + 16] = nn(swap, block).astype(BF16).reshape(16, 16, D)
    pl.semaphore_wait(barrier, len(greeted))

    holder = c == xl
    mine16 = pl.ds(pl.multiple_of(LOCAL * tm, LOCAL), LOCAL)

    @pl.when(jnp.logical_not(holder))
    def _():
        send(raw.at[c], raw.at[c], raw_send.at[0], raw_sem.at[0], partner)
        selections(sel_slice, sel_chunk, sel_rest)

    @pl.when(holder)
    def _():
        wait_bytes(raw.at[1 - c], raw_sem.at[0])
        combine(raw, own_w)
        for h in range(2):
            for n, rows in ((0, share(h, z)), (1, rest(h))):
                src, dst = own_w.at[rows], wbuf.at[mine8, rows]
                pltpu.make_async_copy(src, dst, w1_sem.at[h, n]).start()
                for a in range(2):
                    for b in range(4):
                        if (a, b) != (0, 0):
                            send(src, dst, w_send.at[n], w1_sem.at[h, n], peer(a, b, 0))

    for p in range(3):
        for tx, rx, sem in ((tok_tx, x, x_sem), (dout_tx, g, g_sem)):
            pltpu.make_async_copy(tx.at[3 * tm + p], rx.at[p, mine16], sem.at[p]).start()
            for o in peers:
                target = peer(*o)
                send(tx.at[3 * target["tm"] + p], rx.at[p, mine16], a_send.at[0], sem.at[p], target)

    @pl.when(holder)
    def _():
        selections(sel_slice, sel_chunk, sel_rest)

    ours, theirs4 = pl.ds(4 * c, 4), pl.ds(4 * (1 - c), 4)

    def block_of(rows):
        return wbuf.at[ours, rows]

    def pass_on(rows, ssem, rsem, target):
        send(block_of(rows), block_of(rows), ssem, rsem, target)

    for h in range(2):
        for n, rows in ((0, share(h, z)), (1, rest(h))):
            wait_bytes(block_of(rows), w1_sem.at[h, n])

        pass_on(share(h, z), w_send.at[2], up_sem.at[0, h], ring(1))
        pass_on(share(h, z), w_send.at[3], dn_sem.at[0, h], ring(-1))
        pass_on(share(h, z), w_send.at[4], wcore_sem.at[h], partner)
        pass_on(rest(h), w_send.at[5], wcore_sem.at[h], partner)
    for k in range(1, 5):
        for h in range(2):
            for n, sem, way in ((0, up_sem, 1), (1, dn_sem, -1)):
                q = lax.rem(z - way * k + 8, 8)
                rows = share(h, q) if k < 4 else pl.ds(pl.multiple_of(1296 * h + 160 * q + 80 * n, 16), 80)
                wait_bytes(block_of(rows), sem.at[k - 1, h])
                if k < 3:
                    pass_on(rows, w_send.at[2 + n], sem.at[k, h], ring(way))
                elif k == 3:
                    part = pl.ds(pl.multiple_of(1296 * h + 160 * q + 80 * n, 16), 80)
                    pass_on(part, w_send.at[6 + n], sem.at[k, h], ring(way))
                pass_on(rows, w_send.at[4], wcore_sem.at[h], partner)
            if k == 4:
                wait_bytes(wbuf.at[theirs4, pl.ds(1296 * h, 1296)], wcore_sem.at[h])
                prep_weights(h, wbuf, wt)

    scale, gate = scale_ref[...], gate_ref[...]

    def to_other(*pairs):
        for n, src, dst in pairs:
            send(src, dst, core_send.at[n], core_sem.at[n], partner)

    for p in range(3):
        cols = pl.ds(FR * p, FR)
        wait_bytes(x.at[p], x_sem.at[p])
        wait_bytes(g.at[p], g_sem.at[p])
        inv = patch_front(p, x, g, scale, gate, wt, mod_ref, bg_ref, mod_flip, bg_flip, pt, ot, unit_ref)

        @pl.when(c == 0)
        def _():
            to_other(
                (0, mod_flip.at[:, cols], mod_flip_rx.at[:, cols]), (1, bg_flip.at[:, cols], bg_flip_rx.at[:, cols])
            )

        @pl.when(c == 1)
        def _():
            to_other((0, mod_ref.at[cols], mod_rx.at[cols]), (1, bg_ref.at[cols], bg_rx.at[cols]))

        for h in range(HEADS):
            head_step(h, p, pt, ot, dp, at)

        @pl.when(c == 0)
        def _():
            to_other(
                (2, dp.at[pl.ds(960, 960), cols], dp_rx.at[:, cols]), (3, at.at[pl.ds(320, 320), cols], at_rx.at[:, cols])
            )

        @pl.when(c == 1)
        def _():
            to_other(
                (2, dp.at[pl.ds(0, 960), cols], dp_rx.at[:, cols]), (3, at.at[pl.ds(0, 320), cols], at_rx.at[:, cols])
            )

        patch_end(p, g, scale, wt, dp, unit_ref, inv, dtok)
        pltpu.make_async_copy(dtok.at[p, mine16], back.at[3 * tm + p], back_sem.at[0]).start()
        for o in peers:
            target = peer(*o)
            theirs = pl.ds(pl.multiple_of(LOCAL * target["tm"], LOCAL), LOCAL)
            send(dtok.at[p, theirs], back.at[3 * tm + p], back_send.at[0], back_sem.at[0], target)

    offsets = (4, 3, -3, 2, -2, 1, -1, 0)
    ks = [lax.rem(z + o + 8, 8) for o in offsets]
    blocks = [lax.rem(lax.div(mine8, 2) + i, 4) for i in range(4)]
    ours_l, theirs_l = pl.ds(0, ROWS), pl.ds(ROWS, ROWS)

    def piece(slot):
        return dw.at[pl.ds(144 * slot, 144)]

    def row_piece(u):
        return dw.at[pl.ds(pl.multiple_of(144 * u, 16), 144)]

    def add_piece(ref, got):
        ref[...] = add(ref[...], got[...])

    def ship(src, dst, own, target):
        @pl.when(own)
        def _():
            pltpu.make_async_copy(src, dst, last_sem.at[0]).start()

        @pl.when(jnp.logical_not(own))
        def _():
            send(src, dst, last_send.at[0], last_sem.at[0], target)

    @pl.when(c == 0)
    def _():
        pack_by_column(ks, ours_l, dp, at, l1, l2)
        for n, ref in enumerate((mod_rx, bg_rx, dp_rx, at_rx)):
            wait_bytes(ref, core_sem.at[n])
        pack_by_column(ks, theirs_l, dp_rx, at_rx, l1, l2)
        for slot in range(8):
            if slot % 4 == 0:
                grads_by_column(slot // 4, l1, l2, (mod_ref, mod_rx), (bg_ref, bg_rx), dw)
            for way in range(2):
                for step in range(4):
                    if slot == offsets.index((4 - step) * (1 - 2 * way)) if step else slot == 0:
                        for part in range(2):
                            n = 4 * way + step
                            rows = pl.ds(80 * part, 80 - 16 * part)
                            own = dw.at[pl.ds(144 * slot + 80 * part, 80 - 16 * part)]
                            if step >= 2 or (step == 1 and part == way):
                                wait_bytes(rs_rx.at[n - 1, rows], rs_sem.at[n - 1, part])
                                add_piece(own, rs_rx.at[n - 1, rows])
                            if step or part == way:
                                send(own, rs_rx.at[n, rows], rs_send.at[n], rs_sem.at[n, part], ring(1 - 2 * way))
        for part in range(2):
            for n in (3, 7):
                wait_bytes(rs_rx.at[n, pl.ds(80 * part, 80 - 16 * part)], rs_sem.at[n, part])
        own = piece(7)
        own[...] = (own[...].astype(F32) + rs_rx[3].astype(F32) + rs_rx[7].astype(F32)).astype(BF16)
        for t in range(16):
            lo = slice_window(t)
            last_tx[t, 0:80, :] = nt(sel_slice[t], dw[1008:1136, lo : lo + 256]).astype(BF16)
            last_tx[t, 80:96, 0:80] = nt(dw[1136:1152, lo : lo + 256], sel_slice[t]).astype(BF16)
            ship(
                last_tx.at[t], last_rx.at[xh * 8 + mine8],
                jnp.logical_and(xh == 0, tm == t), {"tm": t, "dp": z},
            )
        for n in (0, 4):
            rows = pl.ds(20 * n, 80 - 4 * n)
            wait_bytes(rs_rx.at[n, rows], rs_send.at[n])
        for n in (1, 2, 3, 5, 6, 7):
            wait_bytes(rs_rx.at[n], rs_send.at[n])

    @pl.when(c == 1)
    def _():
        pack_columns(960, ours_l, dp, 320, at, l1, l2)
        for n, ref in enumerate((mod_flip_rx, bg_flip_rx, dp_rx, at_rx)):
            wait_bytes(ref, core_sem.at[n])
        pack_columns(0, theirs_l, dp_rx, 0, at_rx, l1, l2)
        for i in range(4):
            grads_by_row(blocks[i], l1, l2, (mod_flip, mod_flip_rx), (bg_flip, bg_flip_rx), dw)
            for e in range(2):
                u = 2 * blocks[i] + e

                @pl.when(u == mine8)
                def _():
                    pltpu.make_async_copy(row_piece(u), rs_rx.at[mine8], rs_sem.at[0, 0]).start()

                @pl.when(u != mine8)
                def _():
                    send(row_piece(u), rs_rx.at[mine8], rs_send.at[0], rs_sem.at[0, 0], {"tm": 2 * u + 1, "dp": dpi})

        wait_bytes(rs_rx, rs_sem.at[0, 0])
        total = rs_rx[0].astype(F32)
        for i in range(1, 8):
            total = total + rs_rx[i].astype(F32)
        r, cl = grid2((160, 144))
        split = onehot((lax.rem(r, 80) < HEAD) & (cl == lax.div(r, 80) * HEAD + lax.rem(r, 80)))
        both = nn(split, total.astype(BF16)).astype(BF16)
        for k in range(8):
            lo1, lo2 = column_windows(k)
            pair = jnp.concatenate([both[:, lo1 : lo1 + 256], both[:, lo2 : lo2 + 256]], axis=1)
            out = nn(pair, sel_chunk[k]).astype(BF16)
            for cc in range(2):
                last_tx[2 * k + cc, 0:80, :] = out[80 * cc : 80 * cc + 80]
                last_tx[2 * k + cc, 80:96, 0:80] = nt(sel_rest[k], pair[80 * cc : 80 * cc + 80, 256:512]).astype(BF16)
                ship(
                    last_tx.at[2 * k + cc], last_rx.at[xh * 8 + z],
                    jnp.logical_and(jnp.logical_and(xh == 1, z == k), cc == 1),
                    {"tm": 2 * mine8 + cc, "dp": 8 + k},
                )
        wait_bytes(rs_rx.at[pl.ds(0, 7)], rs_send.at[0])

    @pl.when(c == xh)
    def _():
        wait_bytes(last_tx.at[pl.ds(0, 15)], last_send.at[0])

    @pl.when(c != xh)
    def _():
        wait_bytes(last_tx, last_send.at[0])

    wait_bytes(back, back_sem.at[0])
    for b in range(3):
        block = back[16 * b : 16 * b + 16].reshape(256, D)
        staged[:, 16 * b : 16 * b + 16, :] = nn(swap, block).astype(BF16).reshape(LOCAL, 16, D)
    result = pltpu.make_async_copy(staged, out, out_sem.at[0])
    result.start()

    wait_bytes(last_rx, last_sem.at[0])
    total = last_rx[0].astype(F32)
    for i in range(1, 16):
        total = total + last_rx[i].astype(F32)
    total = total * GRAD_SCALE
    dwq[...] = total[0:HEAD, 0:108]
    dwo[:, 0:20] = total[0:HEAD, 108:128]
    dwo[:, 20:36] = jnp.transpose(total[80:96, :])[0:HEAD, :]

    result.wait()
    wait_bytes(tok_tx.at[pl.ds(0, 45)], a_send.at[0])
    wait_bytes(tok_tx.at[pl.ds(0, 45)], a_send.at[0])
    wait_bytes(tok_tx.at[pl.ds(0, 45)], back_send.at[0])

    for cc, refs in enumerate(((mod_flip_rx, bg_flip_rx, dp_rx, at_rx), (mod_rx, bg_rx, dp_rx, at_rx))):

        @pl.when(c == cc)
        def _():
            for n, ref in enumerate(refs):
                wait_bytes(ref, core_send.at[n])


    @pl.when(holder)
    def _():
        wait_bytes(wbuf.at[pl.ds(0, 7), pl.ds(0, 320)], w_send.at[0])
        wait_bytes(wbuf.at[pl.ds(0, 7), pl.ds(0, 32)], w_send.at[1])

    @pl.when(jnp.logical_not(holder))
    def _():
        wait_bytes(raw.at[c], raw_send.at[0])

    for n, count in ((2, 960), (3, 960), (4, 2560), (5, 32), (6, 160), (7, 160)):
        wait_bytes(wbuf.at[pl.ds(0, 4), pl.ds(0, count)], w_send.at[n])


def main_call(tok, dout, wq, wo, scale, gate):
    vmem, anyspace = pl.BlockSpec(memory_space=pltpu.VMEM), pl.BlockSpec(memory_space=pl.ANY)
    dma = pltpu.SemaphoreType.DMA
    rows3 = pltpu.VMEM((3, FR, D), BF16)
    sent = pltpu.VMEM((PATCH, LOCAL, D), BF16)
    by_row, by_feature = pltpu.VMEM((ROWS, D), BF16), pltpu.VMEM((D, ROWS), BF16)
    return pl.pallas_call(
        main_kernel,
        out_shape=(
            jax.ShapeDtypeStruct((LOCAL, PATCH, D), BF16),
            jax.ShapeDtypeStruct((HEAD, 108), F32),
            jax.ShapeDtypeStruct((HEAD, 36), F32),
        ),
        in_specs=[anyspace, anyspace, vmem, vmem, vmem, vmem],
        out_specs=(anyspace, vmem, vmem),
        scratch_shapes=[
            pltpu.VMEM((LOCAL, PATCH, D), BF16), sent, sent, rows3, rows3,
            pltpu.VMEM((2, PADDED, 128 * TILES), BF16), pltpu.VMEM((144 * TILES, 128), BF16), pltpu.VMEM((8, 144 * TILES, 128), BF16),
            pltpu.VMEM((D, D), BF16), pltpu.VMEM((QR + OR, D), BF16),
            by_row, by_row, by_feature, by_feature,
            pltpu.VMEM((QR, FR), BF16), pltpu.VMEM((OR, FR), BF16),
            pltpu.VMEM((QR, ROWS), BF16), pltpu.VMEM((OR, ROWS), BF16), pltpu.VMEM((FR, D), F32),
            pltpu.VMEM((896, 2 * ROWS), BF16), pltpu.VMEM((384, 2 * ROWS), BF16), rows3, sent,
            by_row, by_row, by_feature, by_feature, pltpu.VMEM((960, ROWS), BF16), pltpu.VMEM((320, ROWS), BF16),
            pltpu.VMEM((8, 144, D), BF16), pltpu.VMEM((16, 80, 256), BF16), pltpu.VMEM((8, 512, 128), BF16),
            pltpu.VMEM((8, 16, 256), BF16), pltpu.VMEM((16, 96, 128), BF16), pltpu.VMEM((16, 96, 128), BF16),
            dma((2,)), dma((1,)), dma((1,)), dma((8,)), dma((2, 2)), dma((4, 2)), dma((4, 2)), dma((2,)),
            dma((1,)), dma((3,)), dma((3,)), dma((1,)), dma((1,)),
            dma((1,)), dma((4,)), dma((4,)), dma((8,)), dma((8, 2)), dma((1,)), dma((1,)),
        ],
        compiler_params=pltpu.CompilerParams(
            collective_id=0, has_side_effects=True, vmem_limit_bytes=62 << 20
        ),
        name="main",
    )(tok, dout, wq, wo, scale, gate)


def shards(tokens, mod_scale, mod_gate, w_qkv, w_out, d_out):
    grads, dwq, dwo = main_call(tokens[0], d_out[0], w_qkv, w_out, mod_scale, mod_gate)
    return grads[None], dwq, dwo


def solution(mesh):
    return jax.shard_map(
        shards,
        mesh=mesh,
        in_specs=(
            P("dp", "tm", None, None),
            P("dp", None),
            P("dp", None),
            P("tm", None),
            P("tm", None),
            P("dp", "tm", None, None),
        ),
        out_specs=(P("dp", "tm", None, None), P("tm", "dp"), P("tm", "dp")),
        check_vma=False,
    )
```

```python
import math

import jax
import jax.numpy as jnp
from jax import lax
from jax.experimental import pallas as pl
from jax.experimental.pallas import tpu as pltpu
from jax.sharding import PartitionSpec as P

F32, BF16 = jnp.float32, jnp.bfloat16
MESH = pl.DeviceIdType.MESH
HEADS, HEAD, PADDED = 8, 72, 80
EPS = 1e-6
D, FR, PATCH, LOCAL = 1152, 256, 48, 16
FACTOR = 1.0 / math.sqrt(HEAD)
EXP2 = FACTOR * math.log2(math.e)
OR = HEADS * PADDED
QR = 3 * OR
ROWS = 768
GRAD_SCALE = 1.0 / math.sqrt(16 * 256 * 48)
TILES = 18


def nn(a, b):
    return lax.dot_general(a, b, (((1,), (0,)), ((), ())), preferred_element_type=F32)


def nt(a, b):
    return lax.dot_general(a, b, (((1,), (1,)), ((), ())), preferred_element_type=F32)


def tn(a, b):
    return lax.dot_general(a, b, (((0,), (0,)), ((), ())), preferred_element_type=F32)


def grid2(shape):
    return lax.broadcasted_iota(jnp.int32, shape, 0), lax.broadcasted_iota(jnp.int32, shape, 1)


def padded(r):
    return lax.div(r, HEAD) * PADDED + lax.rem(r, HEAD)


def onehot(cond):
    return jnp.where(cond, 1.0, 0.0).astype(BF16)


def swap_matrix():
    r, c = grid2((256, 256))
    return onehot(c == lax.rem(r, 16) * 16 + lax.div(r, 16))


def combine(raw, own_w):
    r, c = grid2((144, 160))
    sel = onehot(c == padded(r))
    for i in range(TILES // 2):
        block = jnp.concatenate([raw[core, :, 256 * i : 256 * i + 256] for core in range(2)], axis=0)
        out = nn(sel, block).astype(BF16)
        for k in range(2):
            own_w[288 * i + 144 * k : 288 * i + 144 * k + 144, :] = out[:, 128 * k : 128 * k + 128]


def prep_weights(half, wbuf, wt):
    r, c = grid2((160, 256))
    d = lax.rem(r, PADDED)
    target = lax.div(r, PADDED) * HEAD + d
    for j in range(8 * half, 8 * half + 8):
        tile = (144 * j) // 128
        e = onehot((d < HEAD) & (c == target + (144 * j - 128 * tile)))
        block = jnp.concatenate(
            [
                jnp.concatenate([wbuf[u, 144 * t : 144 * t + 144, :] for t in (tile, tile + 1)], axis=1)
                for u in range(8)
            ],
            axis=0,
        )
        wt[160 * j : 160 * j + 160, :] = nt(e, block).astype(BF16)


def head_step(h, p, pt, ot, dp, at):
    def rows(base):
        return pl.ds(pl.multiple_of(base + PADDED * h, 16), PADDED)

    cols = pl.ds(pl.multiple_of(p * FR, FR), FR)
    q, k, v, o = pt[rows(0), :], pt[rows(OR), :], pt[rows(2 * OR), :], ot[rows(0), :]
    s = tn(k, q)
    top = jnp.max(s, axis=0, keepdims=True)
    e = jnp.exp2((s - top) * EXP2)
    probs = e * (1.0 / jnp.sum(e, axis=0, keepdims=True))
    low = probs.astype(BF16)
    pg = tn(v, o)
    ds = (probs * (pg - jnp.sum(probs * pg, axis=0, keepdims=True))).astype(BF16)
    at[rows(0), cols] = nn(v, low).astype(BF16)
    dp[rows(0), cols] = (nn(k, ds) * FACTOR).astype(BF16)
    dp[rows(OR), cols] = (nt(q, ds) * FACTOR).astype(BF16)
    dp[rows(2 * OR), cols] = nt(o, low).astype(BF16)


def flip(dst, src, cols):
    eye = onehot(jnp.equal(*grid2((256, 256))))
    for lo in range(0, D, 256):
        n = min(256, D - lo)
        dst[lo : lo + n, cols] = nt(eye[:n, :n], src[:, lo : lo + n]).astype(BF16)


def patch_norm(p, x, g, scale, gate, mod_ref, bg_ref, mod_flip, bg_flip):
    rows = pl.ds(FR * p, FR)
    values = x[p].astype(F32)
    mean = jnp.mean(values, axis=-1, keepdims=True)
    cen = values - mean
    inv = lax.rsqrt(jnp.mean(cen * cen, axis=-1, keepdims=True) + EPS)
    mod = (cen * inv * (1.0 + scale)).astype(BF16)
    mod_ref[rows, :] = mod
    flip(mod_flip, mod, rows)
    bg = (g[p].astype(F32) * gate).astype(BF16)
    bg_ref[rows, :] = bg
    flip(bg_flip, bg, rows)
    return mean, inv


def patch_end(p, x, scale, wt, dp, stats, out):
    mean, inv = stats
    ug = tn(dp[:, pl.ds(FR * p, FR)], wt[0:QR, :]) * (1.0 + scale)
    unit = (x[p].astype(F32) - mean) * inv
    branch = inv * (
        ug - jnp.mean(ug, axis=-1, keepdims=True) - unit * jnp.mean(ug * unit, axis=-1, keepdims=True)
    )
    out[p] = branch.astype(BF16)


def pack_by_column(ks, cols, dp, at, l1, l2):
    r, c = grid2((112, 160))
    r2, c2 = grid2((48, 80))
    for i, k in enumerate(ks):
        odd, half = lax.rem(k, 2), lax.div(k, 2)
        sel = onehot((r < 108) & (c == padded(r + 36 * odd)))
        rows = pl.ds(pl.multiple_of(240 * half + 80 * odd, 16), 160)
        l1[112 * i : 112 * i + 112, cols] = nn(sel, dp[rows, :]).astype(BF16)
        sel = onehot((r2 >= 12) & (c2 == r2 - 12 + 36 * odd))
        rows = pl.ds(pl.multiple_of(80 * half, 16), 80)
        l2[48 * i : 48 * i + 48, cols] = nn(sel, at[rows, :]).astype(BF16)


def grads_by_column(group, l1, l2, mods, bgs, dw):
    a_rows, b_rows = pl.ds(448 * group, 448), pl.ds(192 * group, 192)
    t1 = nn(l1[a_rows, 0:ROWS], mods[0][...]) + nn(l1[a_rows, ROWS:], mods[1][...])
    t2 = nn(l2[b_rows, 0:ROWS], bgs[0][...]) + nn(l2[b_rows, ROWS:], bgs[1][...])
    for i in range(4):
        a, b, row = t1[112 * i : 112 * i + 112], t2[48 * i : 48 * i + 48], 144 * (4 * group + i)
        dw[row : row + 96, :] = a[0:96].astype(BF16)
        dw[row + 96 : row + 112, :] = (a[96:112] + b[0:16]).astype(BF16)
        dw[row + 112 : row + 144, :] = b[16:48].astype(BF16)


def pack_columns(first, cols, dp, first_at, at, lb1, lb2):
    r, c = grid2((144, 160))
    sel = onehot(c == padded(r))
    for i in range(6):
        lo = first + 160 * i
        lb1[144 * i : 144 * i + 144, cols] = nn(sel, dp[lo : lo + 160, :]).astype(BF16)
    lb1[864:896, cols] = jnp.zeros((32, ROWS), BF16)
    lb2[0:96, cols] = jnp.zeros((96, ROWS), BF16)
    for i in range(2):
        lo = first_at + 160 * i
        lb2[96 + 144 * i : 240 + 144 * i, cols] = nn(sel, at[lo : lo + 160, :]).astype(BF16)


def grads_by_row(block, lb1, lb2, mods, bgs, dw):
    rows = pl.ds(pl.multiple_of(288 * block, 16), 288)
    a = nt(mods[0][rows, :], lb1[:, 0:ROWS]) + nt(mods[1][rows, :], lb1[:, ROWS:])
    b = nt(bgs[0][rows, :], lb2[:, 0:ROWS]) + nt(bgs[1][rows, :], lb2[:, ROWS:])
    dw[rows, 0:768] = a[:, 0:768].astype(BF16)
    dw[rows, 768:896] = (a[:, 768:896] + b[:, 0:128]).astype(BF16)
    dw[rows, 896:D] = b[:, 128:384].astype(BF16)


def slice_window(t):
    return min(128 * ((72 * t) // 128), 896)


def column_windows(k):
    return 128 * ((108 * k) // 128), min(128 * ((864 + 36 * k) // 128), 896)


def selections(sel_slice, sel_chunk, sel_rest):
    r, c = grid2((80, 256))
    for t in range(16):
        sel_slice[t] = onehot((r < HEAD) & (c == r + (72 * t - slice_window(t))))
    r, c = grid2((256, 128))
    rt, ct = grid2((16, 256))
    for k in range(8):
        lo1, lo2 = column_windows(k)
        sel_chunk[k, 0:256] = onehot((c < 108) & (r + lo1 == 108 * k + c))
        sel_chunk[k, 256:512] = onehot((c >= 108) & (r + lo2 == 756 + 36 * k + c))
        sel_rest[k] = onehot(ct + lo2 == 756 + 36 * k + 128 + rt)


def add(a, b):
    return (a.astype(F32) + b.astype(F32)).astype(BF16)


def wait_bytes(ref, sem):
    pltpu.make_async_copy(ref, ref, sem).wait()


def main_kernel(
    tok, dout, wq, wo, scale_ref, gate_ref,
    out, dwq, dwo,
    staged, tok_tx, dout_tx, x, g, raw, own_w, wbuf, dw, wt, mod_ref, bg_ref, mod_flip, bg_flip, pt, ot, dp, at,
    l1, l2, dtok, back, mod_rx, bg_rx, mod_flip_rx, bg_flip_rx, dp_rx, at_rx,
    rs_rx, sel_slice, sel_chunk, sel_rest, last_tx, last_rx,
    in_sem, raw_send, raw_sem, w_send, w1_sem, up_sem, dn_sem, wcore_sem, a_send, x_sem, g_sem, back_send, back_sem,
    out_sem, core_send, core_sem, rs_send, rs_sem, last_send, last_sem,
):
    tm, dpi = lax.axis_index("tm"), lax.axis_index("dp")
    xl, y, c = lax.div(tm, 8), lax.rem(lax.div(tm, 2), 4), lax.rem(tm, 2)
    xh, z = lax.div(dpi, 8), lax.rem(dpi, 8)
    mine8 = xl * 4 + y

    def peer(a, b, cc):
        return {"tm": lax.rem(xl + a, 2) * 8 + lax.rem(y + b, 4) * 2 + lax.rem(c + cc, 2), "dp": dpi}

    def ring(step):
        return {"tm": tm, "dp": xh * 8 + lax.rem(z + step + 8, 8)}

    partner = peer(0, 0, 1)
    peers = [(a, b, cc) for a in range(2) for b in range(4) for cc in range(2) if (a, b, cc) != (0, 0, 0)]

    def send(src, dst, ssem, rsem, target):
        copy = pltpu.make_async_remote_copy(
            src_ref=src, dst_ref=dst, send_sem=ssem, recv_sem=rsem, device_id=target, device_id_type=MESH
        )
        copy.start()

    def share(h, q):
        return pl.ds(pl.multiple_of(1296 * h + 160 * q, 16), 160)

    def rest(h):
        return pl.ds(1296 * h + 1280, 16)

    first_in = pltpu.make_async_copy(tok, staged, in_sem.at[0])
    first_in.start()

    barrier = pltpu.get_barrier_semaphore()
    other = {"dp": lax.rem(dpi + 8, 16)}
    greeted = [peer(*o) for o in peers] + [peer(0, 0, 0) | other] + [peer(*o) | other for o in peers]
    for step in range(1, 8):
        for cc in range(2):
            here = {"tm": lax.div(tm, 2) * 2 + lax.rem(c + cc, 2)}
            greeted += [here | {"dp": h * 8 + lax.rem(z + step, 8)} for h in range(2)]
    for target in greeted:
        pl.semaphore_signal(barrier, inc=1, device_id=target, device_id_type=MESH)

    swap = swap_matrix()
    raw[c, 0:HEAD, 0:1728] = wq[...]
    raw[c, 0:HEAD, 1728:2304] = wo[...]
    raw[c, HEAD:PADDED, :] = jnp.zeros((PADDED - HEAD, 2304), BF16)
    for n, tx in enumerate((tok_tx, dout_tx)):
        if n:
            second_in = pltpu.make_async_copy(dout, staged, in_sem.at[1])
            second_in.start()
            second_in.wait()
        else:
            first_in.wait()
        for b in range(3):
            block = staged[:, 16 * b : 16 * b + 16, :].reshape(256, D)
            tx[16 * b : 16 * b + 16] = nn(swap, block).astype(BF16).reshape(16, 16, D)
    pl.semaphore_wait(barrier, len(greeted))

    holder = c == xl
    mine16 = pl.ds(pl.multiple_of(LOCAL * tm, LOCAL), LOCAL)

    @pl.when(jnp.logical_not(holder))
    def _():
        send(raw.at[c], raw.at[c], raw_send.at[0], raw_sem.at[0], partner)

    @pl.when(holder)
    def _():
        wait_bytes(raw.at[1 - c], raw_sem.at[0])
        combine(raw, own_w)
        for h in range(2):
            for n, rows in ((0, share(h, z)), (1, rest(h))):
                src, dst = own_w.at[rows], wbuf.at[mine8, rows]
                pltpu.make_async_copy(src, dst, w1_sem.at[h, n]).start()
                for a in range(2):
                    for b in range(4):
                        if (a, b) != (0, 0):
                            send(src, dst, w_send.at[n], w1_sem.at[h, n], peer(a, b, 0))

    ours, theirs4 = pl.ds(4 * c, 4), pl.ds(4 * (1 - c), 4)

    def block_of(rows):
        return wbuf.at[ours, rows]

    def pass_on(rows, ssem, rsem, target):
        send(block_of(rows), block_of(rows), ssem, rsem, target)

    for h in range(2):
        for n, rows in ((0, share(h, z)), (1, rest(h))):
            wait_bytes(block_of(rows), w1_sem.at[h, n])

        pass_on(share(h, z), w_send.at[2], up_sem.at[0, h], ring(1))
        pass_on(share(h, z), w_send.at[3], dn_sem.at[0, h], ring(-1))
        pass_on(share(h, z), w_send.at[4], wcore_sem.at[h], partner)
        pass_on(rest(h), w_send.at[5], wcore_sem.at[h], partner)
    for p in range(3):
        for tx, rx, sem in ((tok_tx, x, x_sem), (dout_tx, g, g_sem)):
            pltpu.make_async_copy(tx.at[3 * tm + p], rx.at[p, mine16], sem.at[p]).start()
            for o in peers:
                target = peer(*o)
                send(tx.at[3 * target["tm"] + p], rx.at[p, mine16], a_send.at[0], sem.at[p], target)

    selections(sel_slice, sel_chunk, sel_rest)

    scale, gate = scale_ref[...], gate_ref[...]

    def to_other(*pairs):
        for n, src, dst in pairs:
            send(src, dst, core_send.at[n], core_sem.at[n], partner)

    def start_patch(p):
        cols = pl.ds(FR * p, FR)
        wait_bytes(x.at[p], x_sem.at[p])
        wait_bytes(g.at[p], g_sem.at[p])
        stats = patch_norm(p, x, g, scale, gate, mod_ref, bg_ref, mod_flip, bg_flip)

        @pl.when(c == 0)
        def _():
            to_other(
                (0, mod_flip.at[:, cols], mod_flip_rx.at[:, cols]), (1, bg_flip.at[:, cols], bg_flip_rx.at[:, cols])
            )

        @pl.when(c == 1)
        def _():
            to_other((0, mod_ref.at[cols], mod_rx.at[cols]), (1, bg_ref.at[cols], bg_rx.at[cols]))

        return stats

    def mix_patch(p):
        cols = pl.ds(FR * p, FR)
        pt[...] = nt(wt[0:QR, :], mod_ref[cols, :]).astype(BF16)
        ot[...] = nt(wt[QR : QR + OR, :], bg_ref[cols, :]).astype(BF16)
        for h in range(HEADS):
            head_step(h, p, pt, ot, dp, at)

        @pl.when(c == 0)
        def _():
            to_other(
                (2, dp.at[pl.ds(960, 960), cols], dp_rx.at[:, cols]), (3, at.at[pl.ds(320, 320), cols], at_rx.at[:, cols])
            )

        @pl.when(c == 1)
        def _():
            to_other(
                (2, dp.at[pl.ds(0, 960), cols], dp_rx.at[:, cols]), (3, at.at[pl.ds(0, 320), cols], at_rx.at[:, cols])
            )

    def end_patch(p, stats):
        patch_end(p, x, scale, wt, dp, stats, dtok)
        pltpu.make_async_copy(dtok.at[p, mine16], back.at[3 * tm + p], back_sem.at[0]).start()
        for o in peers:
            target = peer(*o)
            theirs = pl.ds(pl.multiple_of(LOCAL * target["tm"], LOCAL), LOCAL)
            send(dtok.at[p, theirs], back.at[3 * tm + p], back_send.at[0], back_sem.at[0], target)

    for k in range(1, 5):
        for h in range(2):
            for n, sem, way in ((0, up_sem, 1), (1, dn_sem, -1)):
                q = lax.rem(z - way * k + 8, 8)
                rows = share(h, q) if k < 4 else pl.ds(pl.multiple_of(1296 * h + 160 * q + 80 * n, 16), 80)
                wait_bytes(block_of(rows), sem.at[k - 1, h])
                if k < 3:
                    pass_on(rows, w_send.at[2 + n], sem.at[k, h], ring(way))
                elif k == 3:
                    part = pl.ds(pl.multiple_of(1296 * h + 160 * q + 80 * n, 16), 80)
                    pass_on(part, w_send.at[6 + n], sem.at[k, h], ring(way))
                pass_on(rows, w_send.at[4], wcore_sem.at[h], partner)
            if k == 3 and h == 1:
                stats0 = start_patch(0)
            if k == 4:
                wait_bytes(wbuf.at[theirs4, pl.ds(1296 * h, 1296)], wcore_sem.at[h])
                prep_weights(h, wbuf, wt)

    mix_patch(0)
    end_patch(0, stats0)
    stats1 = start_patch(1)
    mix_patch(1)
    stats2 = start_patch(2)
    mix_patch(2)
    end_patch(1, stats1)

    offsets = (4, 3, -3, 2, -2, 1, -1, 0)
    ks = [lax.rem(z + o + 8, 8) for o in offsets]
    blocks = [lax.rem(lax.div(mine8, 2) + i, 4) for i in (2, 3, 1, 0)]
    ours_l, theirs_l = pl.ds(0, ROWS), pl.ds(ROWS, ROWS)

    def piece(slot):
        return dw.at[pl.ds(144 * slot, 144)]

    def row_piece(u):
        return dw.at[pl.ds(pl.multiple_of(144 * u, 16), 144)]

    def add_piece(ref, got):
        ref[...] = add(ref[...], got[...])

    def ship(src, dst, own, target):
        @pl.when(own)
        def _():
            pltpu.make_async_copy(src, dst, last_sem.at[0]).start()

        @pl.when(jnp.logical_not(own))
        def _():
            send(src, dst, last_send.at[0], last_sem.at[0], target)

    @pl.when(c == 0)
    def _():
        pack_by_column(ks, ours_l, dp, at, l1, l2)
        for n, ref in enumerate((mod_rx, bg_rx, dp_rx, at_rx)):
            wait_bytes(ref, core_sem.at[n])
        pack_by_column(ks, theirs_l, dp_rx, at_rx, l1, l2)
        for slot in range(8):
            if slot % 4 == 0:
                grads_by_column(slot // 4, l1, l2, (mod_ref, mod_rx), (bg_ref, bg_rx), dw)
            if slot == 4:
                end_patch(2, stats2)
            for way in range(2):
                for step in range(4):
                    if slot == offsets.index((4 - step) * (1 - 2 * way)) if step else slot == 0:
                        for part in range(2):
                            n = 4 * way + step
                            rows = pl.ds(80 * part, 80 - 16 * part)
                            own = dw.at[pl.ds(144 * slot + 80 * part, 80 - 16 * part)]
                            if step >= 2 or (step == 1 and part == way):
                                wait_bytes(rs_rx.at[n - 1, rows], rs_sem.at[n - 1, part])
                                add_piece(own, rs_rx.at[n - 1, rows])
                            if step or part == way:
                                send(own, rs_rx.at[n, rows], rs_send.at[n], rs_sem.at[n, part], ring(1 - 2 * way))
        for part in range(2):
            for n in (3, 7):
                wait_bytes(rs_rx.at[n, pl.ds(80 * part, 80 - 16 * part)], rs_sem.at[n, part])
        own = piece(7)
        own[...] = (own[...].astype(F32) + rs_rx[3].astype(F32) + rs_rx[7].astype(F32)).astype(BF16)
        for t in range(16):
            lo = slice_window(t)
            last_tx[t, 0:80, :] = nt(sel_slice[t], dw[1008:1136, lo : lo + 256]).astype(BF16)
            last_tx[t, 80:96, 0:80] = nt(dw[1136:1152, lo : lo + 256], sel_slice[t]).astype(BF16)
            ship(
                last_tx.at[t], last_rx.at[xh * 8 + mine8],
                jnp.logical_and(xh == 0, tm == t), {"tm": t, "dp": z},
            )
        for n in (0, 4):
            rows = pl.ds(20 * n, 80 - 4 * n)
            wait_bytes(rs_rx.at[n, rows], rs_send.at[n])
        for n in (1, 2, 3, 5, 6, 7):
            wait_bytes(rs_rx.at[n], rs_send.at[n])

    @pl.when(c == 1)
    def _():
        pack_columns(960, ours_l, dp, 320, at, l1, l2)
        for n, ref in enumerate((mod_flip_rx, bg_flip_rx, dp_rx, at_rx)):
            wait_bytes(ref, core_sem.at[n])
        pack_columns(0, theirs_l, dp_rx, 0, at_rx, l1, l2)
        for i in range(4):
            grads_by_row(blocks[i], l1, l2, (mod_flip, mod_flip_rx), (bg_flip, bg_flip_rx), dw)
            for e in range(2):
                u = 2 * blocks[i] + e

                @pl.when(u == mine8)
                def _():
                    pltpu.make_async_copy(row_piece(u), rs_rx.at[mine8], rs_sem.at[0, 0]).start()

                @pl.when(u != mine8)
                def _():
                    send(row_piece(u), rs_rx.at[mine8], rs_send.at[0], rs_sem.at[0, 0], {"tm": 2 * u + 1, "dp": dpi})

        end_patch(2, stats2)
        wait_bytes(rs_rx, rs_sem.at[0, 0])
        total = rs_rx[0].astype(F32)
        for i in range(1, 8):
            total = total + rs_rx[i].astype(F32)
        r, cl = grid2((160, 144))
        split = onehot((lax.rem(r, 80) < HEAD) & (cl == lax.div(r, 80) * HEAD + lax.rem(r, 80)))
        both = nn(split, total.astype(BF16)).astype(BF16)
        for k in range(8):
            lo1, lo2 = column_windows(k)
            pair = jnp.concatenate([both[:, lo1 : lo1 + 256], both[:, lo2 : lo2 + 256]], axis=1)
            out = nn(pair, sel_chunk[k]).astype(BF16)
            for cc in range(2):
                last_tx[2 * k + cc, 0:80, :] = out[80 * cc : 80 * cc + 80]
                last_tx[2 * k + cc, 80:96, 0:80] = nt(sel_rest[k], pair[80 * cc : 80 * cc + 80, 256:512]).astype(BF16)
                ship(
                    last_tx.at[2 * k + cc], last_rx.at[xh * 8 + z],
                    jnp.logical_and(jnp.logical_and(xh == 1, z == k), cc == 1),
                    {"tm": 2 * mine8 + cc, "dp": 8 + k},
                )
        wait_bytes(rs_rx.at[pl.ds(0, 7)], rs_send.at[0])

    @pl.when(c == xh)
    def _():
        wait_bytes(last_tx.at[pl.ds(0, 15)], last_send.at[0])

    @pl.when(c != xh)
    def _():
        wait_bytes(last_tx, last_send.at[0])

    wait_bytes(back, back_sem.at[0])
    for b in range(3):
        block = back[16 * b : 16 * b + 16].reshape(256, D)
        staged[:, 16 * b : 16 * b + 16, :] = nn(swap, block).astype(BF16).reshape(LOCAL, 16, D)
    result = pltpu.make_async_copy(staged, out, out_sem.at[0])
    result.start()

    wait_bytes(last_rx, last_sem.at[0])
    total = last_rx[0].astype(F32)
    for i in range(1, 16):
        total = total + last_rx[i].astype(F32)
    total = total * GRAD_SCALE
    dwq[...] = total[0:HEAD, 0:108]
    dwo[:, 0:20] = total[0:HEAD, 108:128]
    dwo[:, 20:36] = jnp.transpose(total[80:96, :])[0:HEAD, :]

    result.wait()
    wait_bytes(tok_tx.at[pl.ds(0, 45)], a_send.at[0])
    wait_bytes(tok_tx.at[pl.ds(0, 45)], a_send.at[0])
    wait_bytes(tok_tx.at[pl.ds(0, 45)], back_send.at[0])

    for cc, refs in enumerate(((mod_flip_rx, bg_flip_rx, dp_rx, at_rx), (mod_rx, bg_rx, dp_rx, at_rx))):

        @pl.when(c == cc)
        def _():
            for n, ref in enumerate(refs):
                wait_bytes(ref, core_send.at[n])


    @pl.when(holder)
    def _():
        wait_bytes(wbuf.at[pl.ds(0, 7), pl.ds(0, 320)], w_send.at[0])
        wait_bytes(wbuf.at[pl.ds(0, 7), pl.ds(0, 32)], w_send.at[1])

    @pl.when(jnp.logical_not(holder))
    def _():
        wait_bytes(raw.at[c], raw_send.at[0])

    for n, count in ((2, 960), (3, 960), (4, 2560), (5, 32), (6, 160), (7, 160)):
        wait_bytes(wbuf.at[pl.ds(0, 4), pl.ds(0, count)], w_send.at[n])


def main_call(tok, dout, wq, wo, scale, gate):
    vmem, anyspace = pl.BlockSpec(memory_space=pltpu.VMEM), pl.BlockSpec(memory_space=pl.ANY)
    dma = pltpu.SemaphoreType.DMA
    rows3 = pltpu.VMEM((3, FR, D), BF16)
    sent = pltpu.VMEM((PATCH, LOCAL, D), BF16)
    by_row, by_feature = pltpu.VMEM((ROWS, D), BF16), pltpu.VMEM((D, ROWS), BF16)
    return pl.pallas_call(
        main_kernel,
        out_shape=(
            jax.ShapeDtypeStruct((LOCAL, PATCH, D), BF16),
            jax.ShapeDtypeStruct((HEAD, 108), F32),
            jax.ShapeDtypeStruct((HEAD, 36), F32),
        ),
        in_specs=[anyspace, anyspace, vmem, vmem, vmem, vmem],
        out_specs=(anyspace, vmem, vmem),
        scratch_shapes=[
            pltpu.VMEM((LOCAL, PATCH, D), BF16), sent, sent, rows3, rows3,
            pltpu.VMEM((2, PADDED, 128 * TILES), BF16), pltpu.VMEM((144 * TILES, 128), BF16), pltpu.VMEM((8, 144 * TILES, 128), BF16),
            pltpu.VMEM((D, D), BF16), pltpu.VMEM((QR + OR, D), BF16),
            by_row, by_row, by_feature, by_feature,
            pltpu.VMEM((QR, FR), BF16), pltpu.VMEM((OR, FR), BF16),
            pltpu.VMEM((QR, ROWS), BF16), pltpu.VMEM((OR, ROWS), BF16),
            pltpu.VMEM((896, 2 * ROWS), BF16), pltpu.VMEM((384, 2 * ROWS), BF16), rows3, sent,
            by_row, by_row, by_feature, by_feature, pltpu.VMEM((960, ROWS), BF16), pltpu.VMEM((320, ROWS), BF16),
            pltpu.VMEM((8, 144, D), BF16), pltpu.VMEM((16, 80, 256), BF16), pltpu.VMEM((8, 512, 128), BF16),
            pltpu.VMEM((8, 16, 256), BF16), pltpu.VMEM((16, 96, 128), BF16), pltpu.VMEM((16, 96, 128), BF16),
            dma((2,)), dma((1,)), dma((1,)), dma((8,)), dma((2, 2)), dma((4, 2)), dma((4, 2)), dma((2,)),
            dma((1,)), dma((3,)), dma((3,)), dma((1,)), dma((1,)),
            dma((1,)), dma((4,)), dma((4,)), dma((8,)), dma((8, 2)), dma((1,)), dma((1,)),
        ],
        compiler_params=pltpu.CompilerParams(
            collective_id=0, has_side_effects=True, vmem_limit_bytes=62 << 20
        ),
        name="main",
    )(tok, dout, wq, wo, scale, gate)


def shards(tokens, mod_scale, mod_gate, w_qkv, w_out, d_out):
    grads, dwq, dwo = main_call(tokens[0], d_out[0], w_qkv, w_out, mod_scale, mod_gate)
    grads = (d_out[0].astype(F32) + grads.astype(F32)).astype(BF16)
    return grads[None], dwq, dwo


def solution(mesh):
    return jax.shard_map(
        shards,
        mesh=mesh,
        in_specs=(
            P("dp", "tm", None, None),
            P("dp", None),
            P("dp", None),
            P("tm", None),
            P("tm", None),
            P("dp", "tm", None, None),
        ),
        out_specs=(P("dp", "tm", None, None), P("tm", "dp"), P("tm", "dp")),
        check_vma=False,
    )
```

```python
import math

import jax
import jax.numpy as jnp
from jax import lax
from jax.experimental import pallas as pl
from jax.experimental.pallas import tpu as pltpu
from jax.sharding import PartitionSpec as P

F32, BF16 = jnp.float32, jnp.bfloat16
MESH = pl.DeviceIdType.MESH
HEADS, HEAD, PADDED = 8, 72, 80
EPS = 1e-6
D, FR, PATCH, LOCAL = 1152, 256, 48, 16
FACTOR = 1.0 / math.sqrt(HEAD)
EXP2 = FACTOR * math.log2(math.e)
OR = HEADS * PADDED
QR = 3 * OR
ROWS = 768
GRAD_SCALE = 1.0 / math.sqrt(16 * 256 * 48)
TILES = 18


def nn(a, b):
    return lax.dot_general(a, b, (((1,), (0,)), ((), ())), preferred_element_type=F32)


def nt(a, b):
    return lax.dot_general(a, b, (((1,), (1,)), ((), ())), preferred_element_type=F32)


def tn(a, b):
    return lax.dot_general(a, b, (((0,), (0,)), ((), ())), preferred_element_type=F32)


def grid2(shape):
    return lax.broadcasted_iota(jnp.int32, shape, 0), lax.broadcasted_iota(jnp.int32, shape, 1)


def padded(r):
    return lax.div(r, HEAD) * PADDED + lax.rem(r, HEAD)


def onehot(cond):
    return jnp.where(cond, 1.0, 0.0).astype(BF16)


def swap_matrix():
    r, c = grid2((256, 256))
    return onehot(c == lax.rem(r, 16) * 16 + lax.div(r, 16))


def combine(raw, own_w):
    r, c = grid2((144, 160))
    sel = onehot(c == padded(r))
    for i in range(TILES // 2):
        block = jnp.concatenate([raw[core, :, 256 * i : 256 * i + 256] for core in range(2)], axis=0)
        out = nn(sel, block).astype(BF16)
        for k in range(2):
            own_w[288 * i + 144 * k : 288 * i + 144 * k + 144, :] = out[:, 128 * k : 128 * k + 128]


def prep_weights(half, wbuf, wt):
    r, c = grid2((160, 256))
    d = lax.rem(r, PADDED)
    target = lax.div(r, PADDED) * HEAD + d
    for j in range(8 * half, 8 * half + 8):
        tile = (144 * j) // 128
        e = onehot((d < HEAD) & (c == target + (144 * j - 128 * tile)))
        block = jnp.concatenate(
            [
                jnp.concatenate([wbuf[u, 144 * t : 144 * t + 144, :] for t in (tile, tile + 1)], axis=1)
                for u in range(8)
            ],
            axis=0,
        )
        wt[160 * j : 160 * j + 160, :] = nt(e, block).astype(BF16)


def head_step(h, p, pt, ot, dp, at):
    def rows(base):
        return pl.ds(pl.multiple_of(base + PADDED * h, 16), PADDED)

    cols = pl.ds(pl.multiple_of(p * FR, FR), FR)
    q, k, v, o = pt[rows(0), :], pt[rows(OR), :], pt[rows(2 * OR), :], ot[rows(0), :]
    s = tn(k, q)
    top = jnp.max(s, axis=0, keepdims=True)
    e = jnp.exp2((s - top) * EXP2)
    probs = e * (1.0 / jnp.sum(e, axis=0, keepdims=True))
    low = probs.astype(BF16)
    pg = tn(v, o)
    ds = (probs * (pg - jnp.sum(probs * pg, axis=0, keepdims=True))).astype(BF16)
    at[rows(0), cols] = nn(v, low).astype(BF16)
    dp[rows(0), cols] = (nn(k, ds) * FACTOR).astype(BF16)
    dp[rows(OR), cols] = (nt(q, ds) * FACTOR).astype(BF16)
    dp[rows(2 * OR), cols] = nt(o, low).astype(BF16)


def flip(dst, src, cols):
    eye = onehot(jnp.equal(*grid2((256, 256))))
    for lo in range(0, D, 256):
        n = min(256, D - lo)
        dst[lo : lo + n, cols] = nt(eye[:n, :n], src[:, lo : lo + n]).astype(BF16)


def patch_norm(p, x, g, scale, gate, mod_ref, bg_ref, mod_flip, bg_flip):
    rows = pl.ds(FR * p, FR)
    values = x[p].astype(F32)
    mean = jnp.mean(values, axis=-1, keepdims=True)
    cen = values - mean
    inv = lax.rsqrt(jnp.mean(cen * cen, axis=-1, keepdims=True) + EPS)
    mod = (cen * inv * (1.0 + scale)).astype(BF16)
    mod_ref[rows, :] = mod
    flip(mod_flip, mod, rows)
    bg = (g[p].astype(F32) * gate).astype(BF16)
    bg_ref[rows, :] = bg
    flip(bg_flip, bg, rows)
    return mean, inv


def patch_end(p, x, scale, wt, dp, stats, out):
    mean, inv = stats
    ug = tn(dp[:, pl.ds(FR * p, FR)], wt[0:QR, :]) * (1.0 + scale)
    unit = (x[p].astype(F32) - mean) * inv
    branch = inv * (
        ug - jnp.mean(ug, axis=-1, keepdims=True) - unit * jnp.mean(ug * unit, axis=-1, keepdims=True)
    )
    out[p] = branch.astype(BF16)


def pack_by_column(ks, cols, dp, at, l1, l2):
    r, c = grid2((112, 160))
    r2, c2 = grid2((48, 80))
    for i, k in enumerate(ks):
        odd, half = lax.rem(k, 2), lax.div(k, 2)
        sel = onehot((r < 108) & (c == padded(r + 36 * odd)))
        rows = pl.ds(pl.multiple_of(240 * half + 80 * odd, 16), 160)
        l1[112 * i : 112 * i + 112, cols] = nn(sel, dp[rows, :]).astype(BF16)
        sel = onehot((r2 >= 12) & (c2 == r2 - 12 + 36 * odd))
        rows = pl.ds(pl.multiple_of(80 * half, 16), 80)
        l2[48 * i : 48 * i + 48, cols] = nn(sel, at[rows, :]).astype(BF16)


def grads_by_column(group, l1, l2, mods, bgs, dw):
    a_rows, b_rows = pl.ds(448 * group, 448), pl.ds(192 * group, 192)
    t1 = nn(l1[a_rows, 0:ROWS], mods[0][...]) + nn(l1[a_rows, ROWS:], mods[1][...])
    t2 = nn(l2[b_rows, 0:ROWS], bgs[0][...]) + nn(l2[b_rows, ROWS:], bgs[1][...])
    for i in range(4):
        a, b, row = t1[112 * i : 112 * i + 112], t2[48 * i : 48 * i + 48], 144 * (4 * group + i)
        dw[row : row + 96, :] = a[0:96].astype(BF16)
        dw[row + 96 : row + 112, :] = (a[96:112] + b[0:16]).astype(BF16)
        dw[row + 112 : row + 144, :] = b[16:48].astype(BF16)


def pack_columns(first, cols, dp, first_at, at, lb1, lb2):
    r, c = grid2((144, 160))
    sel = onehot(c == padded(r))
    for i in range(6):
        lo = first + 160 * i
        lb1[144 * i : 144 * i + 144, cols] = nn(sel, dp[lo : lo + 160, :]).astype(BF16)
    lb1[864:896, cols] = jnp.zeros((32, ROWS), BF16)
    lb2[0:96, cols] = jnp.zeros((96, ROWS), BF16)
    for i in range(2):
        lo = first_at + 160 * i
        lb2[96 + 144 * i : 240 + 144 * i, cols] = nn(sel, at[lo : lo + 160, :]).astype(BF16)


def grads_by_row(block, lb1, lb2, mods, bgs, dw):
    rows = pl.ds(pl.multiple_of(288 * block, 16), 288)
    a = nt(mods[0][rows, :], lb1[:, 0:ROWS]) + nt(mods[1][rows, :], lb1[:, ROWS:])
    b = nt(bgs[0][rows, :], lb2[:, 0:ROWS]) + nt(bgs[1][rows, :], lb2[:, ROWS:])
    dw[rows, 0:768] = a[:, 0:768].astype(BF16)
    dw[rows, 768:896] = (a[:, 768:896] + b[:, 0:128]).astype(BF16)
    dw[rows, 896:D] = b[:, 128:384].astype(BF16)


def slice_window(t):
    return min(128 * ((72 * t) // 128), 896)


def column_windows(k):
    return 128 * ((108 * k) // 128), min(128 * ((864 + 36 * k) // 128), 896)


def selections(sel_slice, sel_chunk, sel_rest):
    r, c = grid2((80, 256))
    for t in range(16):
        sel_slice[t] = onehot((r < HEAD) & (c == r + (72 * t - slice_window(t))))
    r, c = grid2((256, 128))
    rt, ct = grid2((16, 256))
    for k in range(8):
        lo1, lo2 = column_windows(k)
        sel_chunk[k, 0:256] = onehot((c < 108) & (r + lo1 == 108 * k + c))
        sel_chunk[k, 256:512] = onehot((c >= 108) & (r + lo2 == 756 + 36 * k + c))
        sel_rest[k] = onehot(ct + lo2 == 756 + 36 * k + 128 + rt)


def add(a, b):
    return (a.astype(F32) + b.astype(F32)).astype(BF16)


def wait_bytes(ref, sem):
    pltpu.make_async_copy(ref, ref, sem).wait()


def main_kernel(
    tok, dout, wq, wo, scale_ref, gate_ref,
    out, dwq, dwo,
    staged, tok_tx, dout_tx, x, g, raw, own_w, wbuf, dw, wt, mod_ref, bg_ref, mod_flip, bg_flip, pt, ot, dp, at,
    l1, l2, dtok, back, mod_rx, bg_rx, mod_flip_rx, bg_flip_rx, dp_rx, at_rx,
    rs_rx, sel_slice, sel_chunk, sel_rest, last_tx, last_rx,
    in_sem, raw_send, raw_sem, w_send, w1_sem, up_sem, dn_sem, wcore_sem, a_send, x_sem, g_sem, back_send, back_sem,
    out_sem, core_send, core_sem, rs_send, rs_sem, last_send, last_sem,
):
    tm, dpi = lax.axis_index("tm"), lax.axis_index("dp")
    xl, y, c = lax.div(tm, 8), lax.rem(lax.div(tm, 2), 4), lax.rem(tm, 2)
    xh, z = lax.div(dpi, 8), lax.rem(dpi, 8)
    mine8 = xl * 4 + y

    def peer(a, b, cc):
        return {"tm": lax.rem(xl + a, 2) * 8 + lax.rem(y + b, 4) * 2 + lax.rem(c + cc, 2), "dp": dpi}

    def ring(step):
        return {"tm": tm, "dp": xh * 8 + lax.rem(z + step + 8, 8)}

    partner = peer(0, 0, 1)
    peers = [(a, b, cc) for a in range(2) for b in range(4) for cc in range(2) if (a, b, cc) != (0, 0, 0)]

    def send(src, dst, ssem, rsem, target):
        copy = pltpu.make_async_remote_copy(
            src_ref=src, dst_ref=dst, send_sem=ssem, recv_sem=rsem, device_id=target, device_id_type=MESH
        )
        copy.start()

    def share(h, q):
        return pl.ds(pl.multiple_of(1296 * h + 160 * q, 16), 160)

    def rest(h):
        return pl.ds(1296 * h + 1280, 16)

    first_in = pltpu.make_async_copy(tok, staged, in_sem.at[0])
    first_in.start()

    barrier = pltpu.get_barrier_semaphore()
    other = {"dp": lax.rem(dpi + 8, 16)}
    greeted = [peer(*o) for o in peers] + [peer(0, 0, 0) | other] + [peer(*o) | other for o in peers]
    for step in range(1, 8):
        for cc in range(2):
            here = {"tm": lax.div(tm, 2) * 2 + lax.rem(c + cc, 2)}
            greeted += [here | {"dp": h * 8 + lax.rem(z + step, 8)} for h in range(2)]
    for target in greeted:
        pl.semaphore_signal(barrier, inc=1, device_id=target, device_id_type=MESH)

    swap = swap_matrix()
    raw[c, 0:HEAD, 0:1728] = wq[...]
    raw[c, 0:HEAD, 1728:2304] = wo[...]
    raw[c, HEAD:PADDED, :] = jnp.zeros((PADDED - HEAD, 2304), BF16)
    pl.semaphore_wait(barrier, len(greeted))

    holder = c == xl
    opposite = lax.rem(z + 4, 8)
    mine16 = pl.ds(pl.multiple_of(LOCAL * tm, LOCAL), LOCAL)

    @pl.when(jnp.logical_not(holder))
    def _():
        send(raw.at[c], raw.at[c], raw_send.at[0], raw_sem.at[0], partner)

    @pl.when(holder)
    def _():
        wait_bytes(raw.at[1 - c], raw_sem.at[0])
        combine(raw, own_w)
        for h in range(2):
            for n, rows in ((0, share(h, z)), (1, rest(h)), (2, share(h, opposite))):
                src, dst = own_w.at[rows], wbuf.at[mine8, rows]
                pltpu.make_async_copy(src, dst, w1_sem.at[h, n]).start()
                for a in range(2):
                    for b in range(4):
                        if (a, b) != (0, 0):
                            send(src, dst, w_send.at[n % 2], w1_sem.at[h, n], peer(a, b, 0))

    for n, tx in enumerate((tok_tx, dout_tx)):
        if n:
            second_in = pltpu.make_async_copy(dout, staged, in_sem.at[1])
            second_in.start()
            second_in.wait()
        else:
            first_in.wait()
        for b in range(3):
            block = staged[:, 16 * b : 16 * b + 16, :].reshape(256, D)
            tx[16 * b : 16 * b + 16] = nn(swap, block).astype(BF16).reshape(16, 16, D)

    ours, theirs4 = pl.ds(4 * c, 4), pl.ds(4 * (1 - c), 4)

    def block_of(rows):
        return wbuf.at[ours, rows]

    def pass_on(rows, ssem, rsem, target):
        send(block_of(rows), block_of(rows), ssem, rsem, target)

    for n, q in ((0, z), (2, opposite)):
        for h in range(2):
            wait_bytes(block_of(share(h, q)), w1_sem.at[h, n])
            pass_on(share(h, q), w_send.at[2], up_sem.at[n // 2, h], ring(1))
            pass_on(share(h, q), w_send.at[3], dn_sem.at[n // 2, h], ring(-1))
            pass_on(share(h, q), w_send.at[4], wcore_sem.at[h], partner)
    for h in range(2):
        wait_bytes(block_of(rest(h)), w1_sem.at[h, 1])
        pass_on(rest(h), w_send.at[5], wcore_sem.at[h], partner)

    for p in range(3):
        for tx, rx, sem in ((tok_tx, x, x_sem), (dout_tx, g, g_sem)):
            pltpu.make_async_copy(tx.at[3 * tm + p], rx.at[p, mine16], sem.at[p]).start()
            for o in peers:
                target = peer(*o)
                send(tx.at[3 * target["tm"] + p], rx.at[p, mine16], a_send.at[0], sem.at[p], target)

    selections(sel_slice, sel_chunk, sel_rest)

    scale, gate = scale_ref[...], gate_ref[...]

    def to_other(*pairs):
        for n, src, dst in pairs:
            send(src, dst, core_send.at[n], core_sem.at[n], partner)

    def start_patch(p):
        cols = pl.ds(FR * p, FR)
        wait_bytes(x.at[p], x_sem.at[p])
        wait_bytes(g.at[p], g_sem.at[p])
        stats = patch_norm(p, x, g, scale, gate, mod_ref, bg_ref, mod_flip, bg_flip)

        @pl.when(c == 0)
        def _():
            to_other(
                (0, mod_flip.at[:, cols], mod_flip_rx.at[:, cols]), (1, bg_flip.at[:, cols], bg_flip_rx.at[:, cols])
            )

        @pl.when(c == 1)
        def _():
            to_other((0, mod_ref.at[cols], mod_rx.at[cols]), (1, bg_ref.at[cols], bg_rx.at[cols]))

        return stats

    def mix_patch(p):
        cols = pl.ds(FR * p, FR)
        pt[...] = nt(wt[0:QR, :], mod_ref[cols, :]).astype(BF16)
        ot[...] = nt(wt[QR : QR + OR, :], bg_ref[cols, :]).astype(BF16)
        for h in range(HEADS):
            head_step(h, p, pt, ot, dp, at)

        @pl.when(c == 0)
        def _():
            to_other(
                (2, dp.at[pl.ds(960, 960), cols], dp_rx.at[:, cols]), (3, at.at[pl.ds(320, 320), cols], at_rx.at[:, cols])
            )

        @pl.when(c == 1)
        def _():
            to_other(
                (2, dp.at[pl.ds(0, 960), cols], dp_rx.at[:, cols]), (3, at.at[pl.ds(0, 320), cols], at_rx.at[:, cols])
            )

    def end_patch(p, stats):
        patch_end(p, x, scale, wt, dp, stats, dtok)
        pltpu.make_async_copy(dtok.at[p, mine16], back.at[3 * tm + p], back_sem.at[0]).start()
        for o in peers:
            target = peer(*o)
            theirs = pl.ds(pl.multiple_of(LOCAL * target["tm"], LOCAL), LOCAL)
            send(dtok.at[p, theirs], back.at[3 * tm + p], back_send.at[0], back_sem.at[0], target)

    for k, steps in ((0, (-1, 1)), (1, (3, -3)), (2, (-2, 2))):
        if k == 2:
            stats0 = start_patch(0)
        for h in range(2):
            for n, sem, way in ((0, up_sem, 1), (1, dn_sem, -1)):
                rows = share(h, lax.rem(z + steps[n] + 8, 8))
                wait_bytes(block_of(rows), sem.at[k, h])
                if k == 0:
                    pass_on(rows, w_send.at[2 + n], sem.at[2, h], ring(way))
                pass_on(rows, w_send.at[4], wcore_sem.at[h], partner)
            if k == 2:
                wait_bytes(wbuf.at[theirs4, pl.ds(1296 * h, 1296)], wcore_sem.at[h])
                prep_weights(h, wbuf, wt)

    mix_patch(0)
    end_patch(0, stats0)
    stats1 = start_patch(1)
    mix_patch(1)
    stats2 = start_patch(2)
    mix_patch(2)
    end_patch(1, stats1)

    offsets = (4, 3, -3, 2, -2, 1, -1, 0)
    ks = [lax.rem(z + o + 8, 8) for o in offsets]
    blocks = [lax.rem(lax.div(mine8, 2) + i, 4) for i in (2, 1, 3, 0)]
    ours_l, theirs_l = pl.ds(0, ROWS), pl.ds(ROWS, ROWS)

    def piece(slot):
        return dw.at[pl.ds(144 * slot, 144)]

    def row_piece(u):
        return dw.at[pl.ds(pl.multiple_of(144 * u, 16), 144)]

    def add_piece(ref, got):
        ref[...] = add(ref[...], got[...])

    def ship(src, dst, own, target):
        @pl.when(own)
        def _():
            pltpu.make_async_copy(src, dst, last_sem.at[0]).start()

        @pl.when(jnp.logical_not(own))
        def _():
            send(src, dst, last_send.at[0], last_sem.at[0], target)

    @pl.when(c == 0)
    def _():
        pack_by_column(ks, ours_l, dp, at, l1, l2)
        for n, ref in enumerate((mod_rx, bg_rx, dp_rx, at_rx)):
            wait_bytes(ref, core_sem.at[n])
        pack_by_column(ks, theirs_l, dp_rx, at_rx, l1, l2)
        for slot in range(8):
            if slot % 4 == 0:
                grads_by_column(slot // 4, l1, l2, (mod_ref, mod_rx), (bg_ref, bg_rx), dw)
            if slot == 4:
                end_patch(2, stats2)
            for way in range(2):
                for step in range(4):
                    if slot == offsets.index((4 - step) * (1 - 2 * way)) if step else slot == 0:
                        for part in range(2):
                            n = 4 * way + step
                            rows = pl.ds(80 * part, 80 - 16 * part)
                            own = dw.at[pl.ds(144 * slot + 80 * part, 80 - 16 * part)]
                            if step >= 2 or (step == 1 and part == way):
                                wait_bytes(rs_rx.at[n - 1, rows], rs_sem.at[n - 1, part])
                                add_piece(own, rs_rx.at[n - 1, rows])
                            if step or part == way:
                                send(own, rs_rx.at[n, rows], rs_send.at[n], rs_sem.at[n, part], ring(1 - 2 * way))
        for part in range(2):
            for n in (3, 7):
                wait_bytes(rs_rx.at[n, pl.ds(80 * part, 80 - 16 * part)], rs_sem.at[n, part])
        own = piece(7)
        own[...] = (own[...].astype(F32) + rs_rx[3].astype(F32) + rs_rx[7].astype(F32)).astype(BF16)
        for t in range(16):
            lo = slice_window(t)
            last_tx[t, 0:80, :] = nt(sel_slice[t], dw[1008:1136, lo : lo + 256]).astype(BF16)
            last_tx[t, 80:96, 0:80] = nt(dw[1136:1152, lo : lo + 256], sel_slice[t]).astype(BF16)
            ship(
                last_tx.at[t], last_rx.at[xh * 8 + mine8],
                jnp.logical_and(xh == 0, tm == t), {"tm": t, "dp": z},
            )
        for n in (0, 4):
            rows = pl.ds(20 * n, 80 - 4 * n)
            wait_bytes(rs_rx.at[n, rows], rs_send.at[n])
        for n in (1, 2, 3, 5, 6, 7):
            wait_bytes(rs_rx.at[n], rs_send.at[n])

    @pl.when(c == 1)
    def _():
        pack_columns(960, ours_l, dp, 320, at, l1, l2)
        for n, ref in enumerate((mod_flip_rx, bg_flip_rx, dp_rx, at_rx)):
            wait_bytes(ref, core_sem.at[n])
        pack_columns(0, theirs_l, dp_rx, 0, at_rx, l1, l2)
        for i in range(4):
            grads_by_row(blocks[i], l1, l2, (mod_flip, mod_flip_rx), (bg_flip, bg_flip_rx), dw)
            for e in range(2):
                u = 2 * blocks[i] + e

                @pl.when(u == mine8)
                def _():
                    pltpu.make_async_copy(row_piece(u), rs_rx.at[mine8], rs_sem.at[0, 0]).start()

                @pl.when(u != mine8)
                def _():
                    send(row_piece(u), rs_rx.at[mine8], rs_send.at[0], rs_sem.at[0, 0], {"tm": 2 * u + 1, "dp": dpi})

        end_patch(2, stats2)
        wait_bytes(rs_rx, rs_sem.at[0, 0])
        total = rs_rx[0].astype(F32)
        for i in range(1, 8):
            total = total + rs_rx[i].astype(F32)
        r, cl = grid2((160, 144))
        split = onehot((lax.rem(r, 80) < HEAD) & (cl == lax.div(r, 80) * HEAD + lax.rem(r, 80)))
        both = nn(split, total.astype(BF16)).astype(BF16)
        for k in range(8):
            lo1, lo2 = column_windows(k)
            pair = jnp.concatenate([both[:, lo1 : lo1 + 256], both[:, lo2 : lo2 + 256]], axis=1)
            out = nn(pair, sel_chunk[k]).astype(BF16)
            for cc in range(2):
                last_tx[2 * k + cc, 0:80, :] = out[80 * cc : 80 * cc + 80]
                last_tx[2 * k + cc, 80:96, 0:80] = nt(sel_rest[k], pair[80 * cc : 80 * cc + 80, 256:512]).astype(BF16)
                ship(
                    last_tx.at[2 * k + cc], last_rx.at[xh * 8 + z],
                    jnp.logical_and(jnp.logical_and(xh == 1, z == k), cc == 1),
                    {"tm": 2 * mine8 + cc, "dp": 8 + k},
                )
        wait_bytes(rs_rx.at[pl.ds(0, 7)], rs_send.at[0])

    @pl.when(c == xh)
    def _():
        wait_bytes(last_tx.at[pl.ds(0, 15)], last_send.at[0])

    @pl.when(c != xh)
    def _():
        wait_bytes(last_tx, last_send.at[0])

    wait_bytes(back, back_sem.at[0])
    for b in range(3):
        block = back[16 * b : 16 * b + 16].reshape(256, D)
        staged[:, 16 * b : 16 * b + 16, :] = nn(swap, block).astype(BF16).reshape(LOCAL, 16, D)
    result = pltpu.make_async_copy(staged, out, out_sem.at[0])
    result.start()

    wait_bytes(last_rx, last_sem.at[0])
    total = last_rx[0].astype(F32)
    for i in range(1, 16):
        total = total + last_rx[i].astype(F32)
    total = total * GRAD_SCALE
    dwq[...] = total[0:HEAD, 0:108]
    dwo[:, 0:20] = total[0:HEAD, 108:128]
    dwo[:, 20:36] = jnp.transpose(total[80:96, :])[0:HEAD, :]

    result.wait()
    wait_bytes(tok_tx.at[pl.ds(0, 45)], a_send.at[0])
    wait_bytes(tok_tx.at[pl.ds(0, 45)], a_send.at[0])
    wait_bytes(tok_tx.at[pl.ds(0, 45)], back_send.at[0])

    for cc, refs in enumerate(((mod_flip_rx, bg_flip_rx, dp_rx, at_rx), (mod_rx, bg_rx, dp_rx, at_rx))):

        @pl.when(c == cc)
        def _():
            for n, ref in enumerate(refs):
                wait_bytes(ref, core_send.at[n])


    @pl.when(holder)
    def _():
        wait_bytes(wbuf.at[pl.ds(0, 7), pl.ds(0, 640)], w_send.at[0])
        wait_bytes(wbuf.at[pl.ds(0, 7), pl.ds(0, 32)], w_send.at[1])

    @pl.when(jnp.logical_not(holder))
    def _():
        wait_bytes(raw.at[c], raw_send.at[0])

    for n, count in ((2, 960), (3, 960), (4, 2560), (5, 32)):
        wait_bytes(wbuf.at[pl.ds(0, 4), pl.ds(0, count)], w_send.at[n])


def main_call(tok, dout, wq, wo, scale, gate):
    vmem, anyspace = pl.BlockSpec(memory_space=pltpu.VMEM), pl.BlockSpec(memory_space=pl.ANY)
    dma = pltpu.SemaphoreType.DMA
    rows3 = pltpu.VMEM((3, FR, D), BF16)
    sent = pltpu.VMEM((PATCH, LOCAL, D), BF16)
    by_row, by_feature = pltpu.VMEM((ROWS, D), BF16), pltpu.VMEM((D, ROWS), BF16)
    return pl.pallas_call(
        main_kernel,
        out_shape=(
            jax.ShapeDtypeStruct((LOCAL, PATCH, D), BF16),
            jax.ShapeDtypeStruct((HEAD, 108), F32),
            jax.ShapeDtypeStruct((HEAD, 36), F32),
        ),
        in_specs=[anyspace, anyspace, vmem, vmem, vmem, vmem],
        out_specs=(anyspace, vmem, vmem),
        scratch_shapes=[
            pltpu.VMEM((LOCAL, PATCH, D), BF16), sent, sent, rows3, rows3,
            pltpu.VMEM((2, PADDED, 128 * TILES), BF16), pltpu.VMEM((144 * TILES, 128), BF16), pltpu.VMEM((8, 144 * TILES, 128), BF16),
            pltpu.VMEM((D, D), BF16), pltpu.VMEM((QR + OR, D), BF16),
            by_row, by_row, by_feature, by_feature,
            pltpu.VMEM((QR, FR), BF16), pltpu.VMEM((OR, FR), BF16),
            pltpu.VMEM((QR, ROWS), BF16), pltpu.VMEM((OR, ROWS), BF16),
            pltpu.VMEM((896, 2 * ROWS), BF16), pltpu.VMEM((384, 2 * ROWS), BF16), rows3, sent,
            by_row, by_row, by_feature, by_feature, pltpu.VMEM((960, ROWS), BF16), pltpu.VMEM((320, ROWS), BF16),
            pltpu.VMEM((8, 144, D), BF16), pltpu.VMEM((16, 80, 256), BF16), pltpu.VMEM((8, 512, 128), BF16),
            pltpu.VMEM((8, 16, 256), BF16), pltpu.VMEM((16, 96, 128), BF16), pltpu.VMEM((16, 96, 128), BF16),
            dma((2,)), dma((1,)), dma((1,)), dma((6,)), dma((2, 3)), dma((3, 2)), dma((3, 2)), dma((2,)),
            dma((1,)), dma((3,)), dma((3,)), dma((1,)), dma((1,)),
            dma((1,)), dma((4,)), dma((4,)), dma((8,)), dma((8, 2)), dma((1,)), dma((1,)),
        ],
        compiler_params=pltpu.CompilerParams(
            collective_id=0, has_side_effects=True, vmem_limit_bytes=62 << 20
        ),
        name="main",
    )(tok, dout, wq, wo, scale, gate)


def shards(tokens, mod_scale, mod_gate, w_qkv, w_out, d_out):
    grads, dwq, dwo = main_call(tokens[0], d_out[0], w_qkv, w_out, mod_scale, mod_gate)
    grads = (d_out[0].astype(F32) + grads.astype(F32)).astype(BF16)
    return grads[None], dwq, dwo


def solution(mesh):
    return jax.shard_map(
        shards,
        mesh=mesh,
        in_specs=(
            P("dp", "tm", None, None),
            P("dp", None),
            P("dp", None),
            P("tm", None),
            P("tm", None),
            P("dp", "tm", None, None),
        ),
        out_specs=(P("dp", "tm", None, None), P("tm", "dp"), P("tm", "dp")),
        check_vma=False,
    )
```
